32 devices in a mesh: leaf: 2 (over y), blk: 16 (over z, x, core).
Axes of the slice: x: 2, y: 2, z: 4, core: 2. Of those that a mesh axis runs over, the one named last changes fastest.
Arguments:
- right_sides: bfloat16 [2, 16, 4, 512, 32], P('leaf', 'blk'), may hold values from -6 to 6
- inverses: bfloat16 [2, 16, 4, 512, 512], P('leaf', 'blk')
- couplings: bfloat16 [2, 16, 3, 256, 512], P('leaf', 'blk'), may hold values from -0.25 to 0.25
- widths: int32 [2, 16, 4], P('leaf', 'blk'), may hold values from 1 to 4, as said below
- targets: int32 [3, 2, 16, 64], replicated, may hold values from 0 to 4095, as said below
Outputs:
- solution: bfloat16 [2, 16, 4, 512, 32], P('leaf', 'blk')
The draws below stay inside these ranges and needn't reach their ends.
Inputs may be any that keep to these rules, and one draw needn't show every extreme that they name: `widths`: at every level some device has 4 live block units. `targets`: every piece names live rows of its target supernode. At level l, with partner group g XOR 2 ** (l % log2(2)), devices (g, j) and (partner, j) together send at most 9 pieces to owners of blk index d, counting both groups. For each such pair of groups there are one blk index h and one of the two groups such that every pair (g, j), (partner, j) sends exactly 9 pieces to index h of that group, all from one of its two devices.
All inputs are finite; a program needn't handle non-finite values.
Results may differ from the reference program's by a relative error of at most 0.012.
Values may be sent and summed in bfloat16 or wider, within the bound.
No kernel may reach another device: no remote copies, remote signals or barrier semaphores. Data moves between devices by JAX's collectives and lax.ppermute only.
A program may use at most 64 MiB of HBM per device.

```python
import math
import jax
import jax.numpy as jnp
import numpy as np

R = 32
BLOCK = 128
SNB = 4
LEVELS = 4
PIECE = 4
PIECES = 64
W = 512
PR = 256
POS = 128
CAP = 9
N_LEAF = 2
N_BLK = 16


def live_table(key):
    base = jax.random.fold_in(key, 11)
    first, second = jax.random.split(base)
    counts = jax.random.randint(first, (N_LEAF, N_BLK, LEVELS), 1, SNB + 1)
    chosen = jax.random.randint(second, (LEVELS,), 0, N_LEAF * N_BLK)
    flat_ids = jnp.arange(N_LEAF * N_BLK).reshape(N_LEAF, N_BLK)
    counts = jnp.where(flat_ids[:, :, None] == chosen[None, None, :], SNB, counts)
    return counts.astype(jnp.int32)


def draw_widths(key, part):
    return live_table(key)


def draw_targets(key, part):
    counts = live_table(key)
    base = jax.random.fold_in(key, 23)
    leaf_bits = N_LEAF.bit_length() - 1
    group_ids = np.arange(N_LEAF, dtype=np.int32)
    pair_slots = (N_BLK - 1) * CAP
    spare = 2 * PIECES - CAP
    layers = []
    for level in range(LEVELS - 1):
        keys = jax.random.split(jax.random.fold_in(base, level), 7)
        shift_bit = level % leaf_bits
        low_ids = group_ids & ~(1 << shift_bit)
        mine_bits = group_ids >> shift_bit & 1
        hot_blk = jax.random.randint(keys[0], (N_LEAF,), 0, N_BLK)[low_ids]
        hot_pick = jax.random.randint(keys[1], (N_LEAF,), 0, 2)[low_ids]
        hot_group = jnp.asarray(low_ids) + hot_pick * (1 << shift_bit)
        heavy = jax.random.randint(keys[2], (N_LEAF, N_BLK), 0, 2)[low_ids]
        perm_keys = jax.random.split(keys[3], N_LEAF * N_BLK)
        perms = jax.vmap(lambda one: jax.random.permutation(one, pair_slots))(perm_keys)
        perms = perms.reshape(N_LEAF, N_BLK, pair_slots)[low_ids][:, :, :spare]
        dest_rest = perms // CAP
        dest_rest = dest_rest + (dest_rest >= hot_blk[:, None, None]).astype(jnp.int32)
        side_rest = jax.random.randint(keys[4], (N_LEAF, N_BLK, spare), 0, 2)[low_ids]
        hot_side = (hot_group != jnp.asarray(group_ids)).astype(jnp.int32)
        hot_dest = jnp.broadcast_to(hot_blk[:, None, None], (N_LEAF, N_BLK, CAP))
        hot_sides = jnp.broadcast_to(hot_side[:, None, None], (N_LEAF, N_BLK, CAP))
        dest_heavy = jnp.concatenate([hot_dest, dest_rest[:, :, :PIECES - CAP]], axis=2)
        side_heavy = jnp.concatenate([hot_sides, side_rest[:, :, :PIECES - CAP]], axis=2)
        dest_light = dest_rest[:, :, PIECES - CAP:]
        side_light = side_rest[:, :, PIECES - CAP:]
        is_heavy = (heavy == jnp.asarray(mine_bits)[:, None])[:, :, None]
        dest_blk = jnp.where(is_heavy, dest_heavy, dest_light)
        side_bit = jnp.where(is_heavy, side_heavy, side_light)
        target_group = jnp.bitwise_xor(jnp.asarray(group_ids)[:, None, None], side_bit * (1 << shift_bit))
        live_rows = counts[target_group, dest_blk, level + 1] * (BLOCK // PIECE)
        row_place = jax.random.randint(keys[5], (N_LEAF, N_BLK, PIECES), 0, live_rows)
        codes = (side_bit * N_BLK + dest_blk) * POS + row_place
        order_keys = jax.random.split(keys[6], N_LEAF * N_BLK)
        orders = jax.vmap(lambda one: jax.random.permutation(one, PIECES))(order_keys).reshape(N_LEAF, N_BLK, PIECES)
        layers.append(jnp.take_along_axis(codes, orders, axis=2))
    return jnp.stack(layers, axis=0).astype(jnp.int32)


def draw_inverses(key, part):
    shape = (N_LEAF, N_BLK, LEVELS, W, W)
    first, second = jax.random.split(key)
    row_ids = jnp.arange(W)
    below = row_ids[:, None] > row_ids[None, :]
    on_diag = row_ids[:, None] == row_ids[None, :]
    lower = jax.random.normal(first, shape, jnp.float32) * (0.35 / math.sqrt(W))
    diagonal = jnp.exp(jax.random.uniform(second, shape[:-1], jnp.float32, math.log(0.6), math.log(1.6)))
    full = jnp.where(below, lower, 0.0) + jnp.where(on_diag, diagonal[..., None], 0.0)
    return full.astype(jnp.bfloat16)


def block_scale(key, shape, shards, least, high):
    loudness, own = 1.0, jax.random.fold_in(key, 6)
    for axis_at, blocks in shards:
        steps = jnp.exp(jax.random.uniform(jax.random.fold_in(own, axis_at), (blocks,), jnp.float32, least / len(shards), high / len(shards)))
        loudness = loudness * jnp.repeat(steps, shape[axis_at] // blocks).reshape([-1 if axis == axis_at else 1 for axis in range(len(shape))])
    return loudness


def centred(key, extent, scale, bound, shards=(), held_as=jnp.bfloat16):
    values = scale * jax.random.normal(key, extent, jnp.float32)
    if shards:
        values = values * block_scale(key, extent, shards, -0.22, 0.18)
    return jnp.clip(values, -bound, bound).astype(held_as)


def setup_inputs(seed: int = 0) -> dict:
    seeds = jax.random.split(jax.random.key(seed), 6)
    right_sides = centred(seeds[0], (N_LEAF, N_BLK, LEVELS, W, R), 1.0, 6.0, ((0, 2), (1, 16)))
    inverses = draw_inverses(jax.random.fold_in(seeds[5], 71), 0)
    couplings = centred(seeds[2], (N_LEAF, N_BLK, LEVELS - 1, PR, W), W ** -0.5, 0.25, ((0, 2), (1, 16)))
    widths = draw_widths(jax.random.fold_in(seeds[5], 71), 0)
    targets = draw_targets(jax.random.fold_in(seeds[5], 71), 0)
    return {"right_sides": right_sides, "inverses": inverses, "couplings": couplings, "widths": widths, "targets": targets}


def decode_codes(code_list):
    side_bit = code_list // (N_BLK * POS)
    dest_blk = (code_list // POS) % N_BLK
    row_place = code_list % POS
    return side_bit, dest_blk, row_place


def reference(right_sides, inverses, couplings, widths, targets):
    leaf_bits = N_LEAF.bit_length() - 1
    row_index = jnp.arange(W, dtype=jnp.int32)
    group_index = jnp.arange(N_LEAF, dtype=jnp.int32)[:, None, None]
    row_masks = []
    for level in range(LEVELS):
        live_rows = widths[:, :, level, None] * BLOCK
        row_masks.append((row_index[None, None, :] < live_rows).astype(jnp.float32)[..., None])
    forward = []
    flat_targets = []
    incoming = None
    for level in range(LEVELS):
        if level == 0:
            residual = right_sides[:, :, 0]
        else:
            residual = (right_sides[:, :, level].astype(jnp.float32) - incoming).astype(jnp.bfloat16)
        product = jnp.einsum("gjab,gjbr->gjar", inverses[:, :, level].astype(jnp.float32), residual.astype(jnp.float32))
        solved = (row_masks[level] * product).astype(jnp.bfloat16)
        forward.append(solved)
        if level + 1 < LEVELS:
            pieces = jnp.einsum("gjab,gjbr->gjar", couplings[:, :, level].astype(jnp.float32), solved.astype(jnp.float32))
            pieces = pieces.astype(jnp.bfloat16).reshape(N_LEAF * N_BLK * PIECES, PIECE * R)
            side_bit, dest_blk, row_place = decode_codes(targets[level])
            target_group = jnp.bitwise_xor(group_index, side_bit * (2 ** (level % leaf_bits)))
            flat_index = ((target_group * N_BLK + dest_blk) * POS + row_place).reshape(-1).astype(jnp.int32)
            flat_targets.append(flat_index)
            summed = jnp.zeros((N_LEAF * N_BLK * POS, PIECE * R), jnp.float32).at[flat_index].add(pieces.astype(jnp.float32))
            incoming = summed.reshape(N_LEAF, N_BLK, W, R)
    solution = [None] * LEVELS
    for level in reversed(range(LEVELS)):
        if level + 1 == LEVELS:
            back_side = forward[level]
        else:
            above_rows = solution[level + 1].reshape(N_LEAF * N_BLK * POS, PIECE * R)
            gathered = above_rows[flat_targets[level]].reshape(N_LEAF, N_BLK, PR, R)
            update = jnp.einsum("gjba,gjbr->gjar", couplings[:, :, level].astype(jnp.float32), gathered.astype(jnp.float32))
            back_side = (forward[level].astype(jnp.float32) - update).astype(jnp.bfloat16)
        masked = row_masks[level] * back_side.astype(jnp.float32)
        product = jnp.einsum("gjba,gjbr->gjar", inverses[:, :, level].astype(jnp.float32), masked)
        solution[level] = (row_masks[level] * product).astype(jnp.bfloat16)
    return jnp.stack(solution, axis=2)
```

```python
import functools

import jax
import jax.numpy as jnp
from jax import lax
from jax.experimental import pallas as pl
from jax.experimental.pallas import tpu as pltpu
from jax.sharding import Mesh, PartitionSpec as P

BLOCK = 128
MESSAGE = 16
LANES = 128
F32 = jnp.float32
BF16 = jnp.bfloat16


def iota(shape, axis):
    return lax.broadcasted_iota(jnp.int32, shape, axis)


def ones_where(condition):
    return jnp.where(condition, 1.0, 0.0).astype(BF16)


def dot(left, right):
    return jnp.dot(left, right, preferred_element_type=F32)


def trans_dot(left, right):
    return lax.dot_general(left, right, (((0,), (0,)), ((), ())), preferred_element_type=F32)


class Sizes:
    def __init__(self, right_sides, couplings, targets, groups, owners):
        self.levels, self.width, self.columns = right_sides.shape[-3:]
        self.rows = couplings.shape[-2]
        self.pieces = targets.shape[-1]
        self.groups, self.owners = groups, owners
        self.leaf_bits = groups.bit_length() - 1
        self.sub = self.rows // self.pieces
        self.places = self.width // self.sub
        self.slots = 2 * owners * MESSAGE
        self.cap = max(3, (2 * self.pieces + owners - 1) // owners + 1)


def live(widths, level, shape, axis):
    return iota(shape, axis) < widths[0, 0, level] * BLOCK


def own_lanes(sizes, rows):
    shape = (rows, LANES)
    return iota(shape, 1) // sizes.columns == iota(shape, 0) % sizes.sub


def keep_own(sizes, value):
    return jnp.where(own_lanes(sizes, value.shape[0]), value, jnp.zeros_like(value))


def spread(sizes, value):
    value = keep_own(sizes, value)
    step = sizes.columns
    while step < LANES:
        value = value + pltpu.roll(value, step, 1)
        step *= 2
    return value


def repeat_columns(sizes, value):
    return jnp.concatenate([value] * (LANES // sizes.columns), axis=1)


def position(sizes, level, where):
    group, owner = where[0], where[1]
    bit = level % sizes.leaf_bits
    return group, owner, bit


def send_slots(sizes, level, where, targets):
    group, owner, bit = position(sizes, level, where)
    count = sizes.pieces
    table = targets[level, group]
    mine = jnp.sum(jnp.where(iota(table.shape, 0) == owner, table, 0), axis=0, keepdims=True)
    key_row = mine // sizes.places
    square = (count, count)
    diagonal = iota(square, 0) == iota(square, 1)
    keys_down = jnp.broadcast_to(key_row, square)
    key_col = jnp.sum(jnp.where(diagonal, keys_down, 0).astype(F32), axis=1, keepdims=True).astype(jnp.int32)
    same = keys_down == key_col
    rank_row = jnp.sum(jnp.where(same & (iota(square, 0) < iota(square, 1)), 1.0, 0.0), axis=0, keepdims=True)
    rank_col = jnp.sum(jnp.where(same & (iota(square, 1) < iota(square, 0)), 1.0, 0.0), axis=1, keepdims=True)

    def slot(key, rank):
        side, dest = key // sizes.owners, key % sizes.owners
        half = jnp.bitwise_xor(side, lax.shift_right_logical(group, bit) & 1)
        return (half * sizes.owners + dest) * MESSAGE + rank.astype(jnp.int32)

    return slot(key_row, rank_row), slot(key_col, rank_col)


def send_rows(sizes, level, where, targets):
    _, slot_col = send_slots(sizes, level, where, targets)
    shape = (sizes.pieces, sizes.rows)
    chosen = iota(shape, 1) // sizes.sub == iota(shape, 0)
    wide = jnp.sum(jnp.where(chosen, slot_col, 0).astype(F32), axis=0, keepdims=True).astype(jnp.int32)
    return ones_where(iota((sizes.slots, sizes.rows), 0) == wide)


def send_columns(sizes, level, where, targets):
    slot_row, _ = send_slots(sizes, level, where, targets)
    shape = (sizes.rows, sizes.pieces)
    chosen = iota(shape, 0) // sizes.sub == iota(shape, 1)
    wide = jnp.sum(jnp.where(chosen, slot_row, 0).astype(F32), axis=1, keepdims=True).astype(jnp.int32)
    return ones_where(iota((sizes.rows, sizes.slots), 1) == wide)


def take_table(sizes, level, where, targets):
    group, owner, bit = position(sizes, level, where)
    own_half = lax.shift_right_logical(group, bit) & 1
    first = group - own_half * 2**bit
    tables = []
    for half in range(2):
        codes = targets[level, first + half * 2**bit]
        wanted = jnp.bitwise_xor(own_half, half) * sizes.owners + owner
        tables.append(jnp.where(codes // sizes.places == wanted, codes % sizes.places + 1, 0))
    place = jnp.concatenate(tables, axis=0).astype(F32)
    square = (sizes.pieces, sizes.pieces)
    earlier = ones_where(iota(square, 0) < iota(square, 1))
    rank = dot(ones_where(place > 0), earlier)
    return place, rank


def take_rows(sizes, level, where, targets):
    place, rank = take_table(sizes, level, where, targets)
    shape = (2 * sizes.owners, sizes.slots)
    offset = iota(shape, 1) - iota(shape, 0) * MESSAGE
    spot = jnp.zeros(shape, F32)
    for each in range(sizes.cap):
        held = jnp.sum(jnp.where(rank == each, place, 0.0), axis=1, keepdims=True)
        spot = jnp.where(offset == each, held, spot)
    spot = jnp.sum(spot, axis=0, keepdims=True).astype(jnp.int32)
    return ones_where(iota((sizes.width, sizes.slots), 0) // sizes.sub + 1 == spot)


def take_columns(sizes, level, where, targets):
    place, rank = take_table(sizes, level, where, targets)
    shape = (sizes.slots, 2 * sizes.owners)
    source = ones_where(iota(shape, 0) // MESSAGE == iota(shape, 1))
    places = dot(source, place.astype(BF16))
    ranks = dot(source, rank.astype(BF16))
    wanted = (iota(places.shape, 0) % MESSAGE).astype(F32)
    spot = jnp.sum(jnp.where(ranks == wanted, places, 0.0), axis=1, keepdims=True).astype(jnp.int32)
    return ones_where(iota((sizes.slots, sizes.width), 1) // sizes.sub + 1 == spot)


def coupled_inverse(sizes, level, widths, inverse, coupling):
    kept = jnp.where(live(widths, level, coupling.shape, 1), coupling, jnp.zeros_like(coupling))
    return dot(kept, inverse).astype(BF16)


def solve_forward(sizes, level, widths, inverse, residual):
    product = dot(inverse, residual)
    return jnp.where(live(widths, level, product.shape, 0), product, 0.0).astype(BF16)


def solve_backward(sizes, level, widths, inverse, side):
    product = trans_dot(inverse, side)
    return jnp.where(live(widths, level, product.shape, 0), product, 0.0)


def start_kernel(sizes, where, widths, right, inverse, coupling, targets, buffer, forward):
    residual = repeat_columns(sizes, right[0, 0, 0])
    solved = solve_forward(sizes, 0, widths, inverse[0, 0, 0], residual)
    pieces = keep_own(sizes, dot(coupling[0, 0, 0], solved).astype(BF16))
    buffer[...] = dot(send_rows(sizes, 0, where, targets), pieces).astype(BF16)
    forward[...] = solved


def up_plan_kernel(sizes, level, where, widths, right, inverse, coupling, targets, after, side, product, sender, taker):
    side[...] = repeat_columns(sizes, right[0, 0, 0])
    product[...] = coupled_inverse(sizes, level, widths, inverse[0, 0, 0], coupling[0, 0, 0])
    sender[...] = send_rows(sizes, level, where, targets)
    taker[...] = take_rows(sizes, level - 1, where, targets)


def up_kernel(sizes, arrived, side, product, sender, taker, buffer, residual):
    incoming = spread(sizes, dot(taker[...], arrived[...]))
    left = (side[...].astype(F32) - incoming).astype(BF16)
    residual[...] = left
    pieces = keep_own(sizes, dot(product[...], left).astype(BF16))
    buffer[...] = dot(sender[...], pieces).astype(BF16)


def top_plan_kernel(sizes, level, where, widths, right, inverse, targets, after, side, product, taker, returner):
    side[...] = repeat_columns(sizes, right[0, 0, 0])
    block = inverse[0, 0, 0]
    kept = jnp.where(live(widths, level, block.shape, 0), block, jnp.zeros_like(block))
    full = trans_dot(block, kept)
    product[...] = jnp.where(live(widths, level, full.shape, 0), full, 0.0).astype(BF16)
    taker[...] = take_rows(sizes, level - 1, where, targets)
    returner[...] = take_columns(sizes, level - 1, where, targets)


def top_kernel(sizes, arrived, side, product, taker, returner, buffer, solved):
    incoming = spread(sizes, dot(taker[...], arrived[...]))
    left = (side[...].astype(F32) - incoming).astype(BF16)
    value = dot(product[...], left).astype(BF16)
    buffer[...] = dot(returner[...], keep_own(sizes, value)).astype(BF16)
    solved[...] = value


def down_plan_kernel(sizes, level, where, widths, inverse, coupling, targets, state, after, side, product, picker, *returner):
    block = inverse[0, 0, 0]
    forward = state[...]
    if level > 0:
        forward = solve_forward(sizes, level, widths, block, forward)
    side[...] = solve_backward(sizes, level, widths, block, forward)
    full = coupled_inverse(sizes, level, widths, block, coupling[0, 0, 0]).T
    product[...] = jnp.where(live(widths, level, full.shape, 0), full, jnp.zeros_like(full))
    picker[...] = send_columns(sizes, level, where, targets)
    if level > 0:
        returner[0][...] = take_columns(sizes, level - 1, where, targets)


def down_kernel(sizes, arrived, side, product, picker, returner, buffer, solved):
    gathered = spread(sizes, dot(picker[...], arrived[...])).astype(BF16)
    value = (side[...] - dot(product[...], gathered)).astype(BF16)
    buffer[...] = dot(returner[...], keep_own(sizes, value)).astype(BF16)
    solved[...] = value


def last_kernel(sizes, arrived, side, product, picker, first, second, third, out):
    gathered = spread(sizes, dot(picker[...], arrived[...])).astype(BF16)
    value = (side[...] - dot(product[...], gathered)).astype(BF16)
    out[0, 0, 0] = value[:, : sizes.columns]
    for level, solved in enumerate((first, second, third)):
        out[0, 0, level + 1] = solved[:, : sizes.columns]


def level_spec(array, level):
    return pl.BlockSpec((1, 1, 1) + array.shape[3:], lambda step: (0, 0, level, 0, 0))


def whole_spec(shape):
    return pl.BlockSpec(shape, lambda step: (0,) * len(shape))


SCALARS = pl.BlockSpec(memory_space=pltpu.SMEM)
ANYWHERE = pl.BlockSpec(memory_space=pl.ANY)


def call(kernel, name, operands, specs, outs, cost):
    return pl.pallas_call(
        kernel,
        grid=(1,),
        in_specs=[whole_spec(one.shape) if spec is None else spec for one, spec in zip(operands, specs)],
        out_specs=[whole_spec(shape) for shape, _ in outs],
        out_shape=[jax.ShapeDtypeStruct(shape, kind) for shape, kind in outs],
        compiler_params=pltpu.CompilerParams(vmem_limit_bytes=24 * 2**20),
        cost_estimate=pl.CostEstimate(flops=cost, bytes_accessed=2**20, transcendentals=0),
        name=name,
    )(*operands)


def shards(leaf_axes, right_sides, inverses, couplings, widths, targets):
    groups = 1
    group = 0
    for axis in leaf_axes:
        groups *= lax.axis_size(axis)
        group = group * lax.axis_size(axis) + lax.axis_index(axis)
    sizes = Sizes(right_sides, couplings, targets, groups, lax.axis_size("blk"))
    where = jnp.stack([group, lax.axis_index("blk")]).astype(jnp.int32)
    width, slots, rows = sizes.width, sizes.slots, sizes.rows
    top = sizes.levels - 1
    vector = ((width, LANES), BF16)
    message = ((slots, LANES), BF16)
    small, large = 10**6, 10**9

    def exchange(buffer, level):
        pair = leaf_axes[len(leaf_axes) - 1 - level % sizes.leaf_bits]
        blocks = buffer.reshape(2 * sizes.owners, MESSAGE, LANES)
        moved = lax.all_to_all(blocks, (pair, "blk"), split_axis=0, concat_axis=0, tiled=True)
        return moved.reshape(slots, LANES)

    buffer, state = call(
        functools.partial(start_kernel, sizes),
        "start",
        (where, widths, right_sides, inverses, couplings, targets),
        (SCALARS, SCALARS, level_spec(right_sides, 0), level_spec(inverses, 0), level_spec(couplings, 0), None),
        (message, vector),
        large,
    )
    states = [state]
    for level in range(1, top):
        plan = call(
            functools.partial(up_plan_kernel, sizes, level),
            f"up_plan_{level}",
            (where, widths, right_sides, inverses, couplings, targets, buffer),
            (
                SCALARS,
                SCALARS,
                level_spec(right_sides, level),
                level_spec(inverses, level),
                level_spec(couplings, level),
                None,
                ANYWHERE,
            ),
            (vector, ((rows, width), BF16), ((slots, rows), BF16), ((width, slots), BF16)),
            large,
        )
        arrived = exchange(buffer, level - 1)
        buffer, state = call(
            functools.partial(up_kernel, sizes),
            f"up_{level}",
            (arrived, *plan),
            (None,) * 5,
            (message, vector),
            small,
        )
        states.append(state)
    plan = call(
        functools.partial(top_plan_kernel, sizes, top),
        "top_plan",
        (where, widths, right_sides, inverses, targets, buffer),
        (SCALARS, SCALARS, level_spec(right_sides, top), level_spec(inverses, top), None, ANYWHERE),
        (vector, ((width, width), BF16), ((width, slots), BF16), ((slots, width), BF16)),
        large,
    )
    arrived = exchange(buffer, top - 1)
    buffer, solved = call(
        functools.partial(top_kernel, sizes),
        "top",
        (arrived, *plan),
        (None,) * 5,
        (message, vector),
        small,
    )
    solution = [solved]
    for level in reversed(range(top)):
        back = (((slots, width), BF16),) if level else ()
        plan = call(
            functools.partial(down_plan_kernel, sizes, level),
            f"down_plan_{level}",
            (where, widths, inverses, couplings, targets, states[level], buffer),
            (SCALARS, SCALARS, level_spec(inverses, level), level_spec(couplings, level), None, None, ANYWHERE),
            (((width, LANES), F32), ((width, rows), BF16), ((rows, slots), BF16), *back),
            large,
        )
        arrived = exchange(buffer, level)
        if level:
            buffer, solved = call(
                functools.partial(down_kernel, sizes),
                f"down_{level}",
                (arrived, *plan),
                (None,) * 5,
                (message, vector),
                small,
            )
            solution.insert(0, solved)
    (out,) = call(
        functools.partial(last_kernel, sizes),
        "last",
        (arrived, *plan, *solution),
        (None,) * (4 + len(solution)),
        ((right_sides.shape, BF16),),
        small,
    )
    return out


def solution(mesh):
    groups, owners = mesh.devices.shape
    bits = groups.bit_length() - 1
    leaf_axes = tuple(f"leaf{bit}" for bit in reversed(range(bits)))
    split = Mesh(mesh.devices.reshape((2,) * bits + (owners,)), leaf_axes + ("blk",))
    return jax.shard_map(
        functools.partial(shards, leaf_axes),
        mesh=split,
        in_specs=(
            P(leaf_axes, "blk", None, None, None),
            P(leaf_axes, "blk", None, None, None),
            P(leaf_axes, "blk", None, None, None),
            P(leaf_axes, "blk", None),
            P(),
        ),
        out_specs=P(leaf_axes, "blk", None, None, None),
        check_vma=False,
    )
```

```python
import functools

import jax
import jax.numpy as jnp
from jax import lax
from jax.experimental import pallas as pl
from jax.experimental.pallas import tpu as pltpu
from jax.sharding import Mesh, PartitionSpec as P

BLOCK = 128
LANES = 128
F32 = jnp.float32
BF16 = jnp.bfloat16


def iota(shape, axis):
    return lax.broadcasted_iota(jnp.int32, shape, axis)


def ones_where(condition):
    return jnp.where(condition, 1.0, 0.0).astype(BF16)


def dot(left, right):
    return jnp.dot(left, right, preferred_element_type=F32)


def trans_dot(left, right):
    return lax.dot_general(left, right, (((0,), (0,)), ((), ())), preferred_element_type=F32)


class Sizes:
    def __init__(self, right_sides, couplings, targets, leaf_axes):
        self.leaf_axes = leaf_axes
        self.owners = lax.axis_size("blk")
        self.levels, self.columns, self.width = right_sides.shape[-3:]
        self.rows = couplings.shape[-2]
        self.pieces = targets.shape[-1]
        self.leaf_bits = len(leaf_axes)
        self.sub = self.rows // self.pieces
        self.places = self.width // self.sub
        self.cap = max(3, (2 * self.pieces + self.owners - 1) // self.owners + 1)
        self.message = self.cap + self.cap % 2
        self.slots = 2 * self.owners * self.message


def live(widths, level, shape, axis):
    return iota(shape, axis) < widths[level] * BLOCK


def own_lanes(sizes, rows):
    shape = (rows, LANES)
    return iota(shape, 1) // sizes.columns == iota(shape, 0) % sizes.sub


def keep_own(sizes, value):
    return jnp.where(own_lanes(sizes, value.shape[0]), value, jnp.zeros_like(value))


def spread(sizes, value):
    value = keep_own(sizes, value)
    step = sizes.columns
    while step < LANES:
        value = value + pltpu.roll(value, step, 1)
        step *= 2
    return value


def repeat_columns(sizes, value):
    return jnp.concatenate([value] * (LANES // sizes.columns), axis=0).T


def position(sizes, level):
    group = 0
    for axis in sizes.leaf_axes:
        group = group * 2 + lax.axis_index(axis)
    return group, lax.axis_index("blk"), level % sizes.leaf_bits


def send_slots(sizes, level, targets):
    group, owner, bit = position(sizes, level)
    count = sizes.pieces
    table = targets[level, group]
    mine = jnp.sum(jnp.where(iota(table.shape, 0) == owner, table, 0), axis=0, keepdims=True)
    key_row = mine // sizes.places
    square = (count, count)
    diagonal = iota(square, 0) == iota(square, 1)
    keys_down = jnp.broadcast_to(key_row, square)
    key_col = jnp.sum(jnp.where(diagonal, keys_down, 0).astype(F32), axis=1, keepdims=True).astype(jnp.int32)
    same = keys_down == key_col
    rank_row = jnp.sum(jnp.where(same & (iota(square, 0) < iota(square, 1)), 1.0, 0.0), axis=0, keepdims=True)
    rank_col = jnp.sum(jnp.where(same & (iota(square, 1) < iota(square, 0)), 1.0, 0.0), axis=1, keepdims=True)

    def slot(key, rank):
        side, dest = key // sizes.owners, key % sizes.owners
        half = jnp.bitwise_xor(side, lax.shift_right_logical(group, bit) & 1)
        return (half * sizes.owners + dest) * sizes.message + rank.astype(jnp.int32)

    return slot(key_row, rank_row), slot(key_col, rank_col)


def send_rows(sizes, level, targets):
    _, slot_col = send_slots(sizes, level, targets)
    shape = (sizes.pieces, sizes.rows)
    chosen = iota(shape, 1) // sizes.sub == iota(shape, 0)
    wide = jnp.sum(jnp.where(chosen, slot_col, 0).astype(F32), axis=0, keepdims=True).astype(jnp.int32)
    return ones_where(iota((sizes.slots, sizes.rows), 0) == wide)


def send_columns(sizes, level, targets):
    slot_row, _ = send_slots(sizes, level, targets)
    shape = (sizes.rows, sizes.pieces)
    chosen = iota(shape, 0) // sizes.sub == iota(shape, 1)
    wide = jnp.sum(jnp.where(chosen, slot_row, 0).astype(F32), axis=1, keepdims=True).astype(jnp.int32)
    return ones_where(iota((sizes.rows, sizes.slots), 1) == wide)


def take_table(sizes, level, targets):
    group, owner, bit = position(sizes, level)
    own_half = lax.shift_right_logical(group, bit) & 1
    first = group - own_half * 2**bit
    tables = []
    for half in range(2):
        codes = targets[level, first + half * 2**bit]
        wanted = jnp.bitwise_xor(own_half, half) * sizes.owners + owner
        tables.append(jnp.where(codes // sizes.places == wanted, codes % sizes.places + 1, 0))
    place = jnp.concatenate(tables, axis=0).astype(F32)
    square = (sizes.pieces, sizes.pieces)
    earlier = ones_where(iota(square, 0) < iota(square, 1))
    rank = dot(ones_where(place > 0), earlier)
    return place, rank


def take_rows(sizes, level, targets):
    place, rank = take_table(sizes, level, targets)
    shape = (2 * sizes.owners, sizes.slots)
    offset = iota(shape, 1) - iota(shape, 0) * sizes.message
    spot = jnp.zeros(shape, F32)
    for each in range(sizes.cap):
        held = jnp.sum(jnp.where(rank == each, place, 0.0), axis=1, keepdims=True)
        spot = jnp.where(offset == each, held, spot)
    spot = jnp.sum(spot, axis=0, keepdims=True).astype(jnp.int32)
    return ones_where(iota((sizes.width, sizes.slots), 0) // sizes.sub + 1 == spot)


def take_columns(sizes, level, targets):
    place, rank = take_table(sizes, level, targets)
    shape = (sizes.slots, 2 * sizes.owners)
    source = ones_where(iota(shape, 0) // sizes.message == iota(shape, 1))
    places = dot(source, place.astype(BF16))
    ranks = dot(source, rank.astype(BF16))
    wanted = (iota(places.shape, 0) % sizes.message).astype(F32)
    spot = jnp.sum(jnp.where(ranks == wanted, places, 0.0), axis=1, keepdims=True).astype(jnp.int32)
    return ones_where(iota((sizes.slots, sizes.width), 1) // sizes.sub + 1 == spot)


def coupled_inverse(sizes, level, widths, inverse, coupling):
    kept = jnp.where(live(widths, level, coupling.shape, 1), coupling, jnp.zeros_like(coupling))
    return dot(kept, inverse).astype(BF16)


def solve_forward(sizes, level, widths, inverse, residual):
    product = dot(inverse, residual)
    return jnp.where(live(widths, level, product.shape, 0), product, 0.0).astype(BF16)


def solve_backward(sizes, level, widths, inverse, side):
    product = trans_dot(inverse, side)
    return jnp.where(live(widths, level, product.shape, 0), product, 0.0)


def fetch(source, target, semaphore):
    copy = pltpu.make_async_copy(source, target, semaphore)
    copy.start()
    return copy


def start_kernel(sizes, right, inverse, coupling, widths, targets, buffer, forward, *scratch):
    right_in, inverse_in, coupling_in, widths_in, targets_in, done = scratch
    copies = [
        fetch(targets.at[pl.ds(0, 1)], targets_in, done.at[0]),
        fetch(right.at[0, 0, 0], right_in, done.at[1]),
        fetch(widths.at[0, 0], widths_in, done.at[2]),
        fetch(inverse.at[0, 0, 0], inverse_in, done.at[3]),
        fetch(coupling.at[0, 0, 0], coupling_in, done.at[4]),
    ]
    copies[0].wait()
    sender = send_rows(sizes, 0, targets_in)
    copies[1].wait()
    residual = repeat_columns(sizes, right_in[...])
    copies[2].wait()
    copies[3].wait()
    solved = solve_forward(sizes, 0, widths_in, inverse_in[...], residual)
    forward[...] = solved
    copies[4].wait()
    pieces = keep_own(sizes, dot(coupling_in[...], solved).astype(BF16))
    buffer[...] = dot(sender, pieces).astype(BF16)


def up_plan_kernel(sizes, right, inverse, coupling, widths, targets, after, *refs):
    top = sizes.levels - 1
    right_in, inverse_in, coupling_in, widths_in, targets_in, done = refs[-6:]
    outs = refs[:-6]
    copies = [
        fetch(targets, targets_in, done.at[0]),
        fetch(right.at[0, 0], right_in, done.at[1]),
        fetch(widths.at[0, 0], widths_in, done.at[2]),
        fetch(inverse.at[0, 0, pl.ds(1, top)], inverse_in, done.at[3]),
        fetch(coupling.at[0, 0, pl.ds(1, top - 1)], coupling_in, done.at[4]),
    ]
    copies[0].wait()
    for level in range(1, top):
        _, _, sender, taker = outs[4 * level - 4 : 4 * level]
        sender[...] = send_rows(sizes, level, targets_in)
        taker[...] = take_rows(sizes, level - 1, targets_in)
    _, _, taker, returner = outs[-4:]
    taker[...] = take_rows(sizes, top - 1, targets_in)
    returner[...] = take_columns(sizes, top - 1, targets_in)
    copies[1].wait()
    for level in range(1, top + 1):
        outs[4 * level - 4][...] = repeat_columns(sizes, right_in[level])
    copies[2].wait()
    copies[3].wait()
    copies[4].wait()
    for level in range(1, top):
        product = coupled_inverse(sizes, level, widths_in, inverse_in[level - 1], coupling_in[level - 1])
        outs[4 * level - 3][...] = product
    block = inverse_in[top - 1]
    kept = jnp.where(live(widths_in, top, block.shape, 0), block, jnp.zeros_like(block))
    full = trans_dot(block, kept)
    outs[-3][...] = jnp.where(live(widths_in, top, full.shape, 0), full, 0.0).astype(BF16)


def up_kernel(sizes, arrived, side, product, sender, taker, buffer, residual):
    incoming = spread(sizes, dot(taker[...], arrived[...]))
    left = (side[...].astype(F32) - incoming).astype(BF16)
    residual[...] = left
    pieces = keep_own(sizes, dot(product[...], left).astype(BF16))
    buffer[...] = dot(sender[...], pieces).astype(BF16)


def top_kernel(sizes, arrived, side, product, taker, returner, buffer, solved):
    incoming = spread(sizes, dot(taker[...], arrived[...]))
    left = (side[...].astype(F32) - incoming).astype(BF16)
    value = dot(product[...], left).astype(BF16)
    buffer[...] = dot(returner[...], keep_own(sizes, value)).astype(BF16)
    solved[...] = value


def down_plan_kernel(sizes, inverse, coupling, widths, targets, after, *refs):
    top = sizes.levels - 1
    inverse_in, coupling_in, widths_in, targets_in, done = refs[-5:]
    states, products, outs = refs[:top], refs[top : 2 * top - 1], refs[2 * top - 1 : -5]
    copies = [
        fetch(targets, targets_in, done.at[0]),
        fetch(widths.at[0, 0], widths_in, done.at[1]),
        fetch(inverse.at[0, 0, pl.ds(0, top)], inverse_in, done.at[2]),
        fetch(coupling.at[0, 0, 0], coupling_in, done.at[3]),
    ]
    copies[0].wait()
    for level in range(top):
        outs[4 * level + 2][...] = send_columns(sizes, level, targets_in)
        if level > 0:
            outs[4 * level + 3 - 4][...] = take_columns(sizes, level - 1, targets_in)
    for copy in copies[1:]:
        copy.wait()
    for level in range(top):
        block = inverse_in[level]
        forward = states[level][...]
        if level > 0:
            forward = solve_forward(sizes, level, widths_in, block, forward)
            full = products[level - 1][...].T
        else:
            full = coupled_inverse(sizes, level, widths_in, block, coupling_in[...]).T
        outs[4 * level][...] = solve_backward(sizes, level, widths_in, block, forward)
        outs[4 * level + 1][...] = jnp.where(live(widths_in, level, full.shape, 0), full, jnp.zeros_like(full))


def down_kernel(sizes, arrived, side, product, picker, returner, buffer, solved):
    gathered = spread(sizes, dot(picker[...], arrived[...])).astype(BF16)
    value = (side[...] - dot(product[...], gathered)).astype(BF16)
    buffer[...] = dot(returner[...], keep_own(sizes, value)).astype(BF16)
    solved[...] = value


def last_kernel(sizes, arrived, side, product, picker, *refs):
    above, out, held, done = refs[:-3], refs[-3], refs[-2], refs[-1]
    count = len(above)
    for level in range(count):
        held[level + 1] = above[level][...].T[: sizes.columns]
    early = fetch(held.at[pl.ds(1, count)], out.at[0, 0, pl.ds(1, count)], done.at[0])
    gathered = spread(sizes, dot(picker[...], arrived[...])).astype(BF16)
    value = (side[...] - dot(product[...], gathered)).astype(BF16)
    held[0] = value.T[: sizes.columns]
    late = fetch(held.at[0], out.at[0, 0, 0], done.at[1])
    early.wait()
    late.wait()


VMEM = pl.BlockSpec(memory_space=pltpu.VMEM)
HBM = pl.BlockSpec(memory_space=pltpu.HBM)


def call(kernel, name, operands, far, outs, cost, scratch=(), out_spec=VMEM):
    held = [pltpu.with_memory_space_constraint(one, pltpu.HBM) for one in operands[:far]]
    operands = (*held, *operands[far:])
    return pl.pallas_call(
        kernel,
        in_specs=[HBM] * far + [VMEM] * (len(operands) - far),
        out_specs=[out_spec] * len(outs),
        out_shape=[jax.ShapeDtypeStruct(shape, kind) for shape, kind in outs],
        scratch_shapes=scratch,
        compiler_params=pltpu.CompilerParams(vmem_limit_bytes=24 * 2**20),
        cost_estimate=pl.CostEstimate(flops=cost, bytes_accessed=2**20, transcendentals=0),
        name=name,
    )(*operands)


def shards(leaf_axes, right_sides, inverses, couplings, widths, targets):
    right_sides = jnp.swapaxes(right_sides, 3, 4)
    sizes = Sizes(right_sides, couplings, targets, leaf_axes)
    width, slots, rows, columns, levels = sizes.width, sizes.slots, sizes.rows, sizes.columns, sizes.levels
    top = levels - 1
    vector = ((width, LANES), BF16)
    message = ((slots, LANES), BF16)
    side = ((width, LANES), F32)
    codes = targets.shape[1:]
    small, large = 10**6, 10**9

    def exchange(buffer, level):
        pair = leaf_axes[len(leaf_axes) - 1 - level % sizes.leaf_bits]
        blocks = buffer.reshape(slots // 2, 2, LANES)
        moved = lax.all_to_all(blocks, (pair, "blk"), split_axis=0, concat_axis=0, tiled=True)
        return moved.reshape(slots, LANES)

    buffer, state = call(
        functools.partial(start_kernel, sizes),
        "start",
        (right_sides, inverses, couplings, widths, targets),
        5,
        (message, vector),
        large,
        (
            pltpu.VMEM((columns, width), BF16),
            pltpu.VMEM((width, width), BF16),
            pltpu.VMEM((rows, width), BF16),
            pltpu.SMEM((levels,), jnp.int32),
            pltpu.VMEM((1, *codes), jnp.int32),
            pltpu.SemaphoreType.DMA((5,)),
        ),
    )
    up_shapes = (vector, ((rows, width), BF16), ((slots, rows), BF16), ((width, slots), BF16))
    top_shapes = (vector, ((width, width), BF16), ((width, slots), BF16), ((slots, width), BF16))
    plan = call(
        functools.partial(up_plan_kernel, sizes),
        "up_plan",
        (right_sides, inverses, couplings, widths, targets, buffer),
        5,
        up_shapes * (top - 1) + top_shapes,
        large,
        (
            pltpu.VMEM((levels, columns, width), BF16),
            pltpu.VMEM((top, width, width), BF16),
            pltpu.VMEM((top - 1, rows, width), BF16),
            pltpu.SMEM((levels,), jnp.int32),
            pltpu.VMEM(targets.shape, jnp.int32),
            pltpu.SemaphoreType.DMA((5,)),
        ),
    )
    states, products = [state], []
    for level in range(1, top):
        arrived = exchange(buffer, level - 1)
        mine = plan[4 * level - 4 : 4 * level]
        buffer, state = call(
            functools.partial(up_kernel, sizes), f"up_{level}", (arrived, *mine), 0, (message, vector), small
        )
        states.append(state)
        products.append(mine[1])
    arrived = exchange(buffer, top - 1)
    buffer, solved = call(
        functools.partial(top_kernel, sizes), "top", (arrived, *plan[-4:]), 0, (message, vector), small
    )
    down_shapes = (side, ((width, rows), BF16), ((rows, slots), BF16))
    plan = call(
        functools.partial(down_plan_kernel, sizes),
        "down_plan",
        (inverses, couplings, widths, targets, buffer, *states, *products),
        4,
        (*down_shapes, ((slots, width), BF16)) * (top - 1) + down_shapes,
        large,
        (
            pltpu.VMEM((top, width, width), BF16),
            pltpu.VMEM((rows, width), BF16),
            pltpu.SMEM((levels,), jnp.int32),
            pltpu.VMEM(targets.shape, jnp.int32),
            pltpu.SemaphoreType.DMA((4,)),
        ),
    )
    above = [solved]
    for level in reversed(range(1, top)):
        arrived = exchange(buffer, level)
        mine = plan[4 * level : 4 * level + 3]
        buffer, solved = call(
            functools.partial(down_kernel, sizes),
            f"down_{level}",
            (arrived, *mine, plan[4 * level - 1]),
            0,
            (message, vector),
            small,
        )
        above.insert(0, solved)
    arrived = exchange(buffer, 0)
    (out,) = call(
        functools.partial(last_kernel, sizes),
        "last",
        (arrived, *plan[:3], *above),
        0,
        ((right_sides.shape, BF16),),
        small,
        (pltpu.VMEM((levels, columns, width), BF16), pltpu.SemaphoreType.DMA((2,))),
        HBM,
    )
    return jnp.swapaxes(out, 3, 4)


def solution(mesh):
    groups, owners = mesh.devices.shape
    bits = groups.bit_length() - 1
    leaf_axes = tuple(f"leaf{bit}" for bit in reversed(range(bits)))
    split = Mesh(mesh.devices.reshape((2,) * bits + (owners,)), leaf_axes + ("blk",))
    return jax.shard_map(
        functools.partial(shards, leaf_axes),
        mesh=split,
        in_specs=(
            P(leaf_axes, "blk", None, None, None),
            P(leaf_axes, "blk", None, None, None),
            P(leaf_axes, "blk", None, None, None),
            P(leaf_axes, "blk", None),
            P(),
        ),
        out_specs=P(leaf_axes, "blk", None, None, None),
        check_vma=False,
    )
```

```python
import functools

import jax
import jax.numpy as jnp
from jax import lax
from jax.experimental import pallas as pl
from jax.experimental.pallas import tpu as pltpu
from jax.sharding import Mesh, PartitionSpec as P

BLOCK = 128
LANES = 128
F32 = jnp.float32
BF16 = jnp.bfloat16


def iota(shape, axis):
    return lax.broadcasted_iota(jnp.int32, shape, axis)


def ones_where(condition):
    return jnp.where(condition, 1.0, 0.0).astype(BF16)


def dot(left, right):
    return jnp.dot(left, right, preferred_element_type=F32)


def trans_dot(left, right):
    return lax.dot_general(left, right, (((0,), (0,)), ((), ())), preferred_element_type=F32)


def over(value, size):
    if size & (size - 1):
        return value // size
    return lax.shift_right_logical(value, size.bit_length() - 1)


def within(value, size):
    if size & (size - 1):
        return value % size
    return jnp.bitwise_and(value, size - 1)


class Sizes:
    def __init__(self, right_sides, couplings, targets, leaf_axes):
        self.leaf_axes = leaf_axes
        self.owners = lax.axis_size("blk")
        self.levels, self.columns, self.width = right_sides.shape[-3:]
        self.rows = couplings.shape[-2]
        self.pieces = targets.shape[-1]
        self.leaf_bits = len(leaf_axes)
        self.sub = self.rows // self.pieces
        self.places = self.width // self.sub
        self.cap = max(3, (2 * self.pieces + self.owners - 1) // self.owners + 1)
        self.message = self.cap + self.cap % 2
        self.slots = 2 * self.owners * self.message


def live(widths, level, shape, axis):
    return iota(shape, axis) < widths[level] * BLOCK


def own_lanes(sizes, rows):
    shape = (rows, LANES)
    return over(iota(shape, 1), sizes.columns) == within(iota(shape, 0), sizes.sub)


def keep_own(sizes, value):
    return jnp.where(own_lanes(sizes, value.shape[0]), value, jnp.zeros_like(value))


def spread(sizes, value):
    value = keep_own(sizes, value)
    step = sizes.columns
    while step < LANES:
        value = value + pltpu.roll(value, step, 1)
        step *= 2
    return value


def repeat_columns(sizes, value):
    return jnp.concatenate([value] * (LANES // sizes.columns), axis=0).T


def position(sizes, level):
    group = 0
    for axis in sizes.leaf_axes:
        group = group * 2 + lax.axis_index(axis)
    return group, lax.axis_index("blk"), level % sizes.leaf_bits


def send_slots(sizes, level, targets):
    group, owner, bit = position(sizes, level)
    count = sizes.pieces
    table = targets[level, group]
    mine = jnp.sum(jnp.where(iota(table.shape, 0) == owner, table, 0), axis=0, keepdims=True)
    square = (count, count)
    keys_down = jnp.broadcast_to(over(mine, sizes.places), square)
    key_col = jnp.sum(jnp.where(iota(square, 0) == iota(square, 1), keys_down, 0).astype(F32), axis=1, keepdims=True)
    key_col = key_col.astype(jnp.int32)
    earlier = (keys_down == key_col) & (iota(square, 1) < iota(square, 0))
    rank = jnp.sum(jnp.where(earlier, 1.0, 0.0), axis=1, keepdims=True).astype(jnp.int32)
    side, dest = over(key_col, sizes.owners), within(key_col, sizes.owners)
    half = jnp.bitwise_xor(side, lax.shift_right_logical(group, bit) & 1)
    slot = (half * sizes.owners + dest) * sizes.message + rank
    shape = (count, sizes.rows)
    chosen = over(iota(shape, 1), sizes.sub) == iota(shape, 0)
    return jnp.sum(jnp.where(chosen, slot, 0).astype(F32), axis=0, keepdims=True).astype(jnp.int32)


def send_matrix(sizes, slots):
    return ones_where(iota((sizes.slots, sizes.rows), 0) == slots)


def take_places(sizes, level, targets):
    group, owner, bit = position(sizes, level)
    own_half = lax.shift_right_logical(group, bit) & 1
    first = group - own_half * 2**bit
    tables = []
    for half in range(2):
        codes = targets[level, first + half * 2**bit]
        wanted = jnp.bitwise_xor(own_half, half) * sizes.owners + owner
        tables.append(jnp.where(over(codes, sizes.places) == wanted, within(codes, sizes.places) + 1, 0))
    place = jnp.concatenate(tables, axis=0).astype(F32)
    square = (sizes.pieces, sizes.pieces)
    earlier = ones_where(iota(square, 0) < iota(square, 1))
    rank = dot(ones_where(place > 0), earlier)
    shape = (2 * sizes.owners, sizes.slots)
    offset = iota(shape, 1) - iota(shape, 0) * sizes.message
    spot = jnp.zeros(shape, F32)
    for each in range(sizes.cap):
        held = jnp.sum(jnp.where(rank == each, place, 0.0), axis=1, keepdims=True)
        spot = jnp.where(offset == each, held, spot)
    return jnp.sum(spot, axis=0, keepdims=True).astype(jnp.int32) - 1


def take_matrix(sizes, places):
    return ones_where(over(iota((sizes.width, sizes.slots), 0), sizes.sub) == places)


def coupled_inverse(sizes, level, widths, inverse, coupling):
    kept = jnp.where(live(widths, level, coupling.shape, 1), coupling, jnp.zeros_like(coupling))
    return dot(kept, inverse).astype(BF16)


def solve_forward(sizes, level, widths, inverse, residual):
    product = dot(inverse, residual)
    return jnp.where(live(widths, level, product.shape, 0), product, 0.0).astype(BF16)


def solve_backward(sizes, level, widths, inverse, side):
    product = trans_dot(inverse, side)
    return jnp.where(live(widths, level, product.shape, 0), product, 0.0)


def fetch(source, target, semaphore):
    copy = pltpu.make_async_copy(source, target, semaphore)
    copy.start()
    return copy


def squared_inverse(sizes, level, widths, inverse):
    kept = jnp.where(live(widths, level, inverse.shape, 0), inverse, jnp.zeros_like(inverse))
    product = trans_dot(inverse, kept)
    return jnp.where(live(widths, level, product.shape, 0), product, 0.0).astype(BF16)


def start_kernel(sizes, right, inverse, coupling, widths, targets, buffer, forward, *scratch):
    right_in, inverse_in, coupling_in, widths_in, targets_in, done = scratch
    copies = [
        fetch(targets.at[pl.ds(0, 1)], targets_in, done.at[0]),
        fetch(right.at[0, 0, 0], right_in, done.at[1]),
        fetch(widths.at[0, 0], widths_in, done.at[2]),
        fetch(inverse.at[0, 0, 0], inverse_in, done.at[3]),
        fetch(coupling.at[0, 0, 0], coupling_in, done.at[4]),
    ]
    copies[0].wait()
    sender = send_matrix(sizes, send_slots(sizes, 0, targets_in))
    copies[1].wait()
    residual = repeat_columns(sizes, right_in[...])
    copies[2].wait()
    copies[3].wait()
    solved = solve_forward(sizes, 0, widths_in, inverse_in[...], residual)
    forward[...] = solved
    copies[4].wait()
    pieces = keep_own(sizes, dot(coupling_in[...], solved).astype(BF16))
    buffer[...] = dot(sender, pieces).astype(BF16)


def plan_kernel(sizes, right, inverse, coupling, widths, targets, forward, *refs):
    top = sizes.levels - 1
    right_in, inverse_in, coupling_in, widths_in, targets_in, done = refs[-6:]
    sends, takes, limits, start = refs[:4]
    sides, squares = refs[4 : 4 + top], refs[4 + top : 4 + 2 * top]
    products = refs[4 + 2 * top : -6]
    copies = [
        fetch(targets, targets_in, done.at[0]),
        fetch(right.at[0, 0], right_in, done.at[1]),
        fetch(widths.at[0, 0], widths_in, done.at[2]),
        fetch(inverse.at[0, 0], inverse_in, done.at[3]),
        fetch(coupling.at[0, 0], coupling_in, done.at[4]),
    ]
    copies[0].wait()
    for level in range(top):
        sends[level] = send_slots(sizes, level, targets_in)
        takes[level] = take_places(sizes, level, targets_in)
    for copy in copies[1:]:
        copy.wait()
    for level in range(sizes.levels):
        limits[level] = jnp.full((1, LANES), widths_in[level] * BLOCK, jnp.int32)
    for level in range(1, top + 1):
        sides[level - 1][...] = repeat_columns(sizes, right_in[level])
        squares[level - 1][...] = squared_inverse(sizes, level, widths_in, inverse_in[level])
    for level in range(top):
        products[level][...] = coupled_inverse(sizes, level, widths_in, inverse_in[level], coupling_in[level])
    start[...] = solve_backward(sizes, 0, widths_in, inverse_in[0], forward[...]).astype(BF16)


def residual_of(sizes, level, arrived, side, takes):
    incoming = spread(sizes, dot(take_matrix(sizes, takes[level - 1]), arrived[...]))
    return (side[...].astype(F32) - incoming).astype(BF16)


def up_kernel(sizes, level, arrived, side, square, product, sends, takes, buffer, start):
    residual = residual_of(sizes, level, arrived, side, takes)
    pieces = keep_own(sizes, dot(product[...], residual).astype(BF16))
    buffer[...] = dot(send_matrix(sizes, sends[level]), pieces).astype(BF16)
    start[...] = dot(square[...], residual).astype(BF16)


def reply(sizes, level, value, takes):
    return trans_dot(take_matrix(sizes, takes[level - 1]), keep_own(sizes, value)).astype(BF16)


def top_kernel(sizes, level, arrived, side, square, takes, buffer, solved):
    residual = residual_of(sizes, level, arrived, side, takes)
    value = dot(square[...], residual).astype(BF16)
    buffer[...] = reply(sizes, level, value, takes)
    solved[...] = value


def solution_of(sizes, level, arrived, start, product, sends, limits):
    gathered = spread(sizes, trans_dot(send_matrix(sizes, sends[level]), arrived[...])).astype(BF16)
    update = trans_dot(product[...], gathered)
    update = jnp.where(iota(update.shape, 0) < limits[level], update, 0.0)
    return (start[...].astype(F32) - update).astype(BF16)


def down_kernel(sizes, level, arrived, start, product, sends, limits, takes, buffer, solved):
    value = solution_of(sizes, level, arrived, start, product, sends, limits)
    buffer[...] = reply(sizes, level, value, takes)
    solved[...] = value


def last_kernel(sizes, arrived, start, product, sends, limits, *refs):
    above, out, held, done = refs[:-3], refs[-3], refs[-2], refs[-1]
    count = len(above)
    for level in range(count):
        held[level + 1] = above[level][...].T[: sizes.columns]
    early = fetch(held.at[pl.ds(1, count)], out.at[0, 0, pl.ds(1, count)], done.at[0])
    held[0] = solution_of(sizes, 0, arrived, start, product, sends, limits).T[: sizes.columns]
    late = fetch(held.at[0], out.at[0, 0, 0], done.at[1])
    early.wait()
    late.wait()


VMEM = pl.BlockSpec(memory_space=pltpu.VMEM)
HBM = pl.BlockSpec(memory_space=pltpu.HBM)


def call(kernel, name, operands, far, outs, cost, scratch=(), out_spec=VMEM):
    held = [pltpu.with_memory_space_constraint(one, pltpu.HBM) for one in operands[:far]]
    operands = (*held, *operands[far:])
    return pl.pallas_call(
        kernel,
        in_specs=[HBM] * far + [VMEM] * (len(operands) - far),
        out_specs=[out_spec] * len(outs),
        out_shape=[jax.ShapeDtypeStruct(shape, kind) for shape, kind in outs],
        scratch_shapes=scratch,
        compiler_params=pltpu.CompilerParams(vmem_limit_bytes=24 * 2**20),
        cost_estimate=pl.CostEstimate(flops=cost, bytes_accessed=2**20, transcendentals=0),
        name=name,
    )(*operands)


def shards(leaf_axes, right_sides, inverses, couplings, widths, targets):
    right_sides = jnp.swapaxes(right_sides, 3, 4)
    sizes = Sizes(right_sides, couplings, targets, leaf_axes)
    width, slots, rows, columns, levels = sizes.width, sizes.slots, sizes.rows, sizes.columns, sizes.levels
    top = levels - 1
    vector = ((width, LANES), BF16)
    message = ((slots, LANES), BF16)
    matrix = ((width, width), BF16)
    coupled = ((rows, width), BF16)
    small, large = 10**6, 10**9

    def exchange(buffer, level):
        pair = leaf_axes[len(leaf_axes) - 1 - level % sizes.leaf_bits]
        blocks = buffer.reshape(slots // 2, 2, LANES)
        moved = lax.all_to_all(blocks, (pair, "blk"), split_axis=0, concat_axis=0, tiled=True)
        return moved.reshape(slots, LANES)

    inputs = (right_sides, inverses, couplings, widths, targets)
    buffer, forward = call(
        functools.partial(start_kernel, sizes),
        "start",
        inputs,
        5,
        (message, vector),
        large,
        (
            pltpu.VMEM((columns, width), BF16),
            pltpu.VMEM((width, width), BF16),
            pltpu.VMEM((rows, width), BF16),
            pltpu.SMEM((levels,), jnp.int32),
            pltpu.VMEM((1, *targets.shape[1:]), jnp.int32),
            pltpu.SemaphoreType.DMA((5,)),
        ),
    )
    sends, takes, limits, start, *planned = call(
        functools.partial(plan_kernel, sizes),
        "plan",
        (*inputs, forward),
        5,
        (
            ((top, 1, rows), jnp.int32),
            ((top, 1, slots), jnp.int32),
            ((levels, 1, LANES), jnp.int32),
            vector,
            *(vector,) * top,
            *(matrix,) * top,
            *(coupled,) * top,
        ),
        large,
        (
            pltpu.VMEM((levels, columns, width), BF16),
            pltpu.VMEM((levels, width, width), BF16),
            pltpu.VMEM((top, rows, width), BF16),
            pltpu.SMEM((levels,), jnp.int32),
            pltpu.VMEM(targets.shape, jnp.int32),
            pltpu.SemaphoreType.DMA((5,)),
        ),
    )
    sides, squares, products = planned[:top], planned[top : 2 * top], planned[2 * top :]
    starts = [start]
    for level in range(1, top):
        arrived = exchange(buffer, level - 1)
        buffer, start = call(
            functools.partial(up_kernel, sizes, level),
            f"up_{level}",
            (arrived, sides[level - 1], squares[level - 1], products[level], sends, takes),
            0,
            (message, vector),
            small,
        )
        starts.append(start)
    arrived = exchange(buffer, top - 1)
    buffer, solved = call(
        functools.partial(top_kernel, sizes, top),
        "top",
        (arrived, sides[-1], squares[-1], takes),
        0,
        (message, vector),
        small,
    )
    above = [solved]
    for level in reversed(range(1, top)):
        arrived = exchange(buffer, level)
        buffer, solved = call(
            functools.partial(down_kernel, sizes, level),
            f"down_{level}",
            (arrived, starts[level], products[level], sends, limits, takes),
            0,
            (message, vector),
            small,
        )
        above.insert(0, solved)
    arrived = exchange(buffer, 0)
    (out,) = call(
        functools.partial(last_kernel, sizes),
        "last",
        (arrived, starts[0], products[0], sends, limits, *above),
        0,
        ((right_sides.shape, BF16),),
        small,
        (pltpu.VMEM((levels, columns, width), BF16), pltpu.SemaphoreType.DMA((2,))),
        HBM,
    )
    return jnp.swapaxes(out, 3, 4)


def solution(mesh):
    groups, owners = mesh.devices.shape
    bits = groups.bit_length() - 1
    leaf_axes = tuple(f"leaf{bit}" for bit in reversed(range(bits)))
    split = Mesh(mesh.devices.reshape((2,) * bits + (owners,)), leaf_axes + ("blk",))
    return jax.shard_map(
        functools.partial(shards, leaf_axes),
        mesh=split,
        in_specs=(
            P(leaf_axes, "blk", None, None, None),
            P(leaf_axes, "blk", None, None, None),
            P(leaf_axes, "blk", None, None, None),
            P(leaf_axes, "blk", None),
            P(),
        ),
        out_specs=P(leaf_axes, "blk", None, None, None),
        check_vma=False,
    )
```

```python
import functools

import jax
import jax.numpy as jnp
from jax import lax
from jax.experimental import pallas as pl
from jax.experimental.pallas import tpu as pltpu
from jax.sharding import Mesh, PartitionSpec as P

BLOCK = 128
LANES = 128
F32 = jnp.float32
BF16 = jnp.bfloat16


def iota(shape, axis):
    return lax.broadcasted_iota(jnp.int32, shape, axis)


def ones_where(condition):
    return jnp.where(condition, 1.0, 0.0).astype(BF16)


def dot(left, right):
    return jnp.dot(left, right, preferred_element_type=F32)


def trans_dot(left, right):
    return lax.dot_general(left, right, (((0,), (0,)), ((), ())), preferred_element_type=F32)


def over(value, size):
    if size & (size - 1):
        return value // size
    return lax.shift_right_logical(value, size.bit_length() - 1)


def within(value, size):
    if size & (size - 1):
        return value % size
    return jnp.bitwise_and(value, size - 1)


class Sizes:
    def __init__(self, right_sides, couplings, targets, leaf_axes):
        self.leaf_axes = leaf_axes
        self.near, self.far = lax.axis_size("near"), lax.axis_size("far")
        self.owners = self.near * self.far
        self.levels, self.columns, self.width = right_sides.shape[-3:]
        self.rows = couplings.shape[-2]
        self.pieces = targets.shape[-1]
        self.leaf_bits = len(leaf_axes)
        self.sub = self.rows // self.pieces
        self.places = self.width // self.sub
        self.cap = max(3, (2 * self.pieces + self.owners - 1) // self.owners + 1)
        self.message = self.cap + self.cap % 2
        self.slots = 2 * self.owners * self.message


def live(limits, level, shape, axis):
    return iota(shape, axis) < limits[level][:, :1]


def own_lanes(sizes, rows):
    shape = (rows, LANES)
    return over(iota(shape, 1), sizes.columns) == within(iota(shape, 0), sizes.sub)


def keep_own(sizes, value):
    return jnp.where(own_lanes(sizes, value.shape[0]), value, jnp.zeros_like(value))


def spread(sizes, value):
    value = keep_own(sizes, value)
    step = sizes.columns
    while step < LANES:
        value = value + pltpu.roll(value, step, 1)
        step *= 2
    return value


def repeat_columns(sizes, value):
    return jnp.concatenate([value] * (LANES // sizes.columns), axis=0).T


def position(sizes, level):
    group = 0
    for axis in sizes.leaf_axes:
        group = group * 2 + lax.axis_index(axis)
    owner = lax.axis_index("far") * sizes.near + lax.axis_index("near")
    return group, owner, level % sizes.leaf_bits


def turn(sizes, half, owner):
    return (within(owner, sizes.near) * 2 + half) * sizes.far + over(owner, sizes.near)


def send_slots(sizes, level, targets):
    group, owner, bit = position(sizes, level)
    count = sizes.pieces
    table = targets[level, group]
    mine = jnp.sum(jnp.where(iota(table.shape, 0) == owner, table, 0), axis=0, keepdims=True)
    square = (count, count)
    keys_down = jnp.broadcast_to(over(mine, sizes.places), square)
    key_col = jnp.sum(jnp.where(iota(square, 0) == iota(square, 1), keys_down, 0).astype(F32), axis=1, keepdims=True)
    key_col = key_col.astype(jnp.int32)
    earlier = (keys_down == key_col) & (iota(square, 1) < iota(square, 0))
    rank = jnp.sum(jnp.where(earlier, 1.0, 0.0), axis=1, keepdims=True).astype(jnp.int32)
    side, dest = over(key_col, sizes.owners), within(key_col, sizes.owners)
    half = jnp.bitwise_xor(side, lax.shift_right_logical(group, bit) & 1)
    slot = turn(sizes, half, dest) * sizes.message + rank
    shape = (count, sizes.rows)
    chosen = over(iota(shape, 1), sizes.sub) == iota(shape, 0)
    return jnp.sum(jnp.where(chosen, slot, 0).astype(F32), axis=0, keepdims=True).astype(jnp.int32)


def send_matrix(sizes, slots):
    return ones_where(iota((sizes.slots, sizes.rows), 0) == slots)


def take_places(sizes, level, targets):
    group, owner, bit = position(sizes, level)
    own_half = lax.shift_right_logical(group, bit) & 1
    first = group - own_half * 2**bit
    tables = []
    for half in range(2):
        codes = targets[level, first + half * 2**bit]
        wanted = jnp.bitwise_xor(own_half, half) * sizes.owners + owner
        tables.append(jnp.where(over(codes, sizes.places) == wanted, within(codes, sizes.places) + 1, 0))
    place = jnp.concatenate(tables, axis=0).astype(F32)
    square = (sizes.pieces, sizes.pieces)
    earlier = ones_where(iota(square, 0) < iota(square, 1))
    rank = dot(ones_where(place > 0), earlier)
    shape = (2 * sizes.owners, sizes.slots)
    source = iota(shape, 0)
    source = turn(sizes, over(source, sizes.owners), within(source, sizes.owners))
    offset = iota(shape, 1) - source * sizes.message
    spot = jnp.zeros(shape, F32)
    for each in range(sizes.cap):
        held = jnp.sum(jnp.where(rank == each, place, 0.0), axis=1, keepdims=True)
        spot = jnp.where(offset == each, held, spot)
    return jnp.sum(spot, axis=0, keepdims=True).astype(jnp.int32) - 1


def take_matrix(sizes, places):
    return ones_where(over(iota((sizes.width, sizes.slots), 0), sizes.sub) == places)


def coupled_inverse(sizes, level, limits, inverse, coupling):
    kept = jnp.where(live(limits, level, coupling.shape, 1), coupling, jnp.zeros_like(coupling))
    return dot(kept, inverse).astype(BF16)


def solve_forward(sizes, level, limits, inverse, residual):
    product = dot(inverse, residual)
    return jnp.where(live(limits, level, product.shape, 0), product, 0.0).astype(BF16)


def solve_backward(sizes, level, limits, inverse, side):
    product = trans_dot(inverse, side)
    return jnp.where(live(limits, level, product.shape, 0), product, 0.0)


def fetch(source, target, semaphore):
    copy = pltpu.make_async_copy(source, target, semaphore)
    copy.start()
    return copy


def squared_inverse(sizes, level, limits, inverse):
    kept = jnp.where(live(limits, level, inverse.shape, 0), inverse, jnp.zeros_like(inverse))
    product = trans_dot(inverse, kept)
    return jnp.where(live(limits, level, product.shape, 0), product, 0.0).astype(BF16)


def start_kernel(sizes, right, inverse, coupling, widths, targets, buffer, forward, limits, *refs):
    right_in, inverse_in, coupling_in, targets_in, widths_in, done = refs
    top = sizes.levels - 1
    first, others = pl.ds(0, 1), pl.ds(1, top)
    copies = [
        fetch(targets, targets_in, done.at[0]),
        fetch(right.at[0, 0], right_in, done.at[1]),
        fetch(widths.at[0, 0], widths_in, done.at[2]),
        fetch(inverse.at[0, 0, first], inverse_in.at[first], done.at[3]),
        fetch(coupling.at[0, 0, first], coupling_in.at[first], done.at[4]),
        fetch(inverse.at[0, 0, others], inverse_in.at[others], done.at[5]),
        fetch(coupling.at[0, 0, pl.ds(1, top - 1)], coupling_in.at[pl.ds(1, top - 1)], done.at[6]),
    ]
    copies[0].wait()
    sender = send_matrix(sizes, send_slots(sizes, 0, targets_in))
    copies[1].wait()
    residual = repeat_columns(sizes, right_in[0])
    copies[2].wait()
    for level in range(sizes.levels):
        limits[level] = jnp.full((1, LANES), widths_in[level] * BLOCK, jnp.int32)
    copies[3].wait()
    solved = solve_forward(sizes, 0, limits, inverse_in[0], residual)
    forward[...] = solved
    copies[4].wait()
    pieces = keep_own(sizes, dot(coupling_in[0], solved).astype(BF16))
    buffer[...] = dot(sender, pieces).astype(BF16)
    copies[5].wait()
    copies[6].wait()


def plan_kernel(sizes, forward, limits, right, inverse, coupling, targets, *refs):
    top = sizes.levels - 1
    sends, takes, start, first, last = refs[:5]
    sides, stacks = refs[5 : 5 + top], refs[5 + top :]
    for level in range(1, top + 1):
        sides[level - 1][...] = repeat_columns(sizes, right[level])
    for level in range(top):
        product = coupled_inverse(sizes, level, limits, inverse[level], coupling[level])
        if level == 0:
            first[...] = product
        else:
            stacks[level - 1][pl.ds(0, sizes.rows)] = product
            stacks[level - 1][pl.ds(sizes.rows, sizes.width)] = squared_inverse(sizes, level, limits, inverse[level])
    last[...] = squared_inverse(sizes, top, limits, inverse[top])
    start[...] = solve_backward(sizes, 0, limits, inverse[0], forward[...]).astype(BF16)
    for level in range(top):
        sends[level] = send_slots(sizes, level, targets)
        takes[level] = take_places(sizes, level, targets)


def residual_of(sizes, level, arrived, side, takes):
    incoming = spread(sizes, dot(take_matrix(sizes, takes[level - 1]), arrived[...]))
    return (side[...].astype(F32) - incoming).astype(BF16)


def up_kernel(sizes, level, arrived, side, stack, sends, takes, buffer, start):
    residual = residual_of(sizes, level, arrived, side, takes)
    both = dot(stack[...], residual)
    pieces = keep_own(sizes, both[: sizes.rows].astype(BF16))
    buffer[...] = dot(send_matrix(sizes, sends[level]), pieces).astype(BF16)
    start[...] = both[sizes.rows :].astype(BF16)


def reply(sizes, level, value, takes):
    return trans_dot(take_matrix(sizes, takes[level - 1]), keep_own(sizes, value)).astype(BF16)


def top_kernel(sizes, level, arrived, side, square, takes, buffer, solved):
    residual = residual_of(sizes, level, arrived, side, takes)
    value = dot(square[...], residual).astype(BF16)
    buffer[...] = reply(sizes, level, value, takes)
    solved[...] = value


def solution_of(sizes, level, arrived, start, product, sends, limits):
    gathered = spread(sizes, trans_dot(send_matrix(sizes, sends[level]), arrived[...])).astype(BF16)
    update = trans_dot(product, gathered)
    update = jnp.where(live(limits, level, update.shape, 0), update, 0.0)
    return (start[...].astype(F32) - update).astype(BF16)


def down_kernel(sizes, level, arrived, start, product, sends, limits, takes, buffer, solved):
    value = solution_of(sizes, level, arrived, start, product[: sizes.rows], sends, limits)
    buffer[...] = reply(sizes, level, value, takes)
    solved[...] = value


def last_kernel(sizes, arrived, start, product, sends, limits, *refs):
    above, out, held, done = refs[:-3], refs[-3], refs[-2], refs[-1]
    count = len(above)
    for level in range(count):
        held[level + 1] = above[level][...].T[: sizes.columns]
    early = fetch(held.at[pl.ds(1, count)], out.at[0, 0, pl.ds(1, count)], done.at[0])
    held[0] = solution_of(sizes, 0, arrived, start, product[...], sends, limits).T[: sizes.columns]
    late = fetch(held.at[0], out.at[0, 0, 0], done.at[1])
    early.wait()
    late.wait()


VMEM = pl.BlockSpec(memory_space=pltpu.VMEM)
HBM = pl.BlockSpec(memory_space=pltpu.HBM)


def call(kernel, name, operands, far, outs, cost, scratch=(), out_spec=VMEM):
    held = [pltpu.with_memory_space_constraint(one, pltpu.HBM) for one in operands[:far]]
    operands = (*held, *operands[far:])
    return pl.pallas_call(
        kernel,
        in_specs=[HBM] * far + [VMEM] * (len(operands) - far),
        out_specs=[out_spec] * len(outs),
        out_shape=[jax.ShapeDtypeStruct(shape, kind) for shape, kind in outs],
        scratch_shapes=scratch,
        compiler_params=pltpu.CompilerParams(vmem_limit_bytes=24 * 2**20),
        cost_estimate=pl.CostEstimate(flops=cost, bytes_accessed=2**20, transcendentals=0),
        name=name,
    )(*operands)


def shards(leaf_axes, right_sides, inverses, couplings, widths, targets):
    right_sides = jnp.swapaxes(right_sides, 3, 4)
    sizes = Sizes(right_sides, couplings, targets, leaf_axes)
    width, slots, rows, columns, levels = sizes.width, sizes.slots, sizes.rows, sizes.columns, sizes.levels
    top = levels - 1
    vector = ((width, LANES), BF16)
    message = ((slots, LANES), BF16)
    matrix = ((width, width), BF16)
    stacked = ((rows + width, width), BF16)
    small, large = 10**6, 10**9

    def exchange(buffer, level):
        pair = leaf_axes[len(leaf_axes) - 1 - level % sizes.leaf_bits]
        blocks = buffer.reshape(slots // 2, 2, LANES)
        moved = lax.all_to_all(blocks, ("near", pair, "far"), split_axis=0, concat_axis=0, tiled=True)
        return moved.reshape(slots, LANES)

    inputs = (right_sides, inverses, couplings, widths, targets)
    buffer, *held = call(
        functools.partial(start_kernel, sizes),
        "start",
        inputs,
        5,
        (
            message,
            vector,
            ((levels, 1, LANES), jnp.int32),
            ((levels, columns, width), BF16),
            ((levels, width, width), BF16),
            ((top, rows, width), BF16),
            (targets.shape, jnp.int32),
        ),
        large,
        (pltpu.SMEM((levels,), jnp.int32), pltpu.SemaphoreType.DMA((7,))),
    )
    limits = held[1]
    sends, takes, start, first, last, *planned = call(
        functools.partial(plan_kernel, sizes),
        "plan",
        held,
        0,
        (
            ((top, 1, rows), jnp.int32),
            ((top, 1, slots), jnp.int32),
            vector,
            ((rows, width), BF16),
            matrix,
            *(vector,) * top,
            *(stacked,) * (top - 1),
        ),
        large,
    )
    sides, stacks = planned[:top], planned[top:]
    starts = [start]
    for level in range(1, top):
        arrived = exchange(buffer, level - 1)
        buffer, start = call(
            functools.partial(up_kernel, sizes, level),
            f"up_{level}",
            (arrived, sides[level - 1], stacks[level - 1], sends, takes),
            0,
            (message, vector),
            small,
        )
        starts.append(start)
    arrived = exchange(buffer, top - 1)
    buffer, solved = call(
        functools.partial(top_kernel, sizes, top),
        "top",
        (arrived, sides[-1], last, takes),
        0,
        (message, vector),
        small,
    )
    above = [solved]
    for level in reversed(range(1, top)):
        arrived = exchange(buffer, level)
        buffer, solved = call(
            functools.partial(down_kernel, sizes, level),
            f"down_{level}",
            (arrived, starts[level], stacks[level - 1], sends, limits, takes),
            0,
            (message, vector),
            small,
        )
        above.insert(0, solved)
    arrived = exchange(buffer, 0)
    (out,) = call(
        functools.partial(last_kernel, sizes),
        "last",
        (arrived, starts[0], first, sends, limits, *above),
        0,
        ((right_sides.shape, BF16),),
        small,
        (pltpu.VMEM((levels, columns, width), BF16), pltpu.SemaphoreType.DMA((2,))),
        HBM,
    )
    return jnp.swapaxes(out, 3, 4)


def solution(mesh):
    groups, owners = mesh.devices.shape
    bits = groups.bit_length() - 1
    near = 1 if owners % 4 else 4
    leaf_axes = tuple(f"leaf{bit}" for bit in reversed(range(bits)))
    split = Mesh(mesh.devices.reshape((2,) * bits + (owners // near, near)), leaf_axes + ("far", "near"))
    blk = ("far", "near")
    return jax.shard_map(
        functools.partial(shards, leaf_axes),
        mesh=split,
        in_specs=(
            P(leaf_axes, blk, None, None, None),
            P(leaf_axes, blk, None, None, None),
            P(leaf_axes, blk, None, None, None),
            P(leaf_axes, blk, None),
            P(),
        ),
        out_specs=P(leaf_axes, blk, None, None, None),
        check_vma=False,
    )
```

```python
import functools

import jax
import jax.numpy as jnp
from jax import lax
from jax.experimental import pallas as pl
from jax.experimental.pallas import tpu as pltpu
from jax.sharding import Mesh, PartitionSpec as P

BLOCK = 128
LANES = 128
F32 = jnp.float32
BF16 = jnp.bfloat16


def iota(shape, axis):
    return lax.broadcasted_iota(jnp.int32, shape, axis)


def ones_where(condition):
    return jnp.where(condition, 1.0, 0.0).astype(BF16)


def dot(left, right):
    return jnp.dot(left, right, preferred_element_type=F32)


def trans_dot(left, right):
    return lax.dot_general(left, right, (((0,), (0,)), ((), ())), preferred_element_type=F32)


def over(value, size):
    if size & (size - 1):
        return value // size
    return lax.shift_right_logical(value, size.bit_length() - 1)


def within(value, size):
    if size & (size - 1):
        return value % size
    return jnp.bitwise_and(value, size - 1)


class Sizes:
    def __init__(self, right_sides, couplings, targets, leaf_axes):
        self.leaf_axes = leaf_axes
        self.near, self.far = lax.axis_size("near"), lax.axis_size("far")
        self.owners = self.near * self.far
        self.levels, self.columns, self.width = right_sides.shape[-3:]
        self.rows = couplings.shape[-2]
        self.pieces = targets.shape[-1]
        self.leaf_bits = len(leaf_axes)
        self.sub = self.rows // self.pieces
        self.places = self.width // self.sub
        self.cap = max(3, (2 * self.pieces + self.owners - 1) // self.owners + 1)
        self.message = self.cap + self.cap % 2
        self.slots = 2 * self.owners * self.message


def live(limits, level, shape, axis):
    return iota(shape, axis) < limits[level][:, :1]


def own_lanes(sizes, rows):
    shape = (rows, LANES)
    return over(iota(shape, 1), sizes.columns) == within(iota(shape, 0), sizes.sub)


def keep_own(sizes, value):
    return jnp.where(own_lanes(sizes, value.shape[0]), value, jnp.zeros_like(value))


def spread(sizes, value):
    value = keep_own(sizes, value)
    step = sizes.columns
    while step < LANES:
        value = value + pltpu.roll(value, step, 1)
        step *= 2
    return value


def repeat_columns(sizes, value):
    return jnp.concatenate([value] * (LANES // sizes.columns), axis=0).T


def position(sizes, level):
    group = 0
    for axis in sizes.leaf_axes:
        group = group * 2 + lax.axis_index(axis)
    owner = lax.axis_index("far") * sizes.near + lax.axis_index("near")
    return group, owner, level % sizes.leaf_bits


def turn(sizes, half, owner):
    return (within(owner, sizes.near) * 2 + half) * sizes.far + over(owner, sizes.near)


def send_slots(sizes, level, targets):
    group, owner, bit = position(sizes, level)
    count = sizes.pieces
    table = targets[level, group]
    mine = jnp.sum(jnp.where(iota(table.shape, 0) == owner, table, 0), axis=0, keepdims=True)
    square = (count, count)
    keys_down = jnp.broadcast_to(over(mine, sizes.places), square)
    key_col = jnp.sum(jnp.where(iota(square, 0) == iota(square, 1), keys_down, 0).astype(F32), axis=1, keepdims=True)
    key_col = key_col.astype(jnp.int32)
    earlier = (keys_down == key_col) & (iota(square, 1) < iota(square, 0))
    rank = jnp.sum(jnp.where(earlier, 1.0, 0.0), axis=1, keepdims=True).astype(jnp.int32)
    side, dest = over(key_col, sizes.owners), within(key_col, sizes.owners)
    half = jnp.bitwise_xor(side, lax.shift_right_logical(group, bit) & 1)
    slot = turn(sizes, half, dest) * sizes.message + rank
    shape = (count, sizes.rows)
    chosen = over(iota(shape, 1), sizes.sub) == iota(shape, 0)
    return jnp.sum(jnp.where(chosen, slot, 0).astype(F32), axis=0, keepdims=True).astype(jnp.int32)


def send_matrix(sizes, slots):
    return ones_where(iota((sizes.slots, sizes.rows), 0) == slots)


def take_places(sizes, level, targets):
    group, owner, bit = position(sizes, level)
    own_half = lax.shift_right_logical(group, bit) & 1
    first = group - own_half * 2**bit
    tables = []
    for half in range(2):
        codes = targets[level, first + half * 2**bit]
        wanted = jnp.bitwise_xor(own_half, half) * sizes.owners + owner
        tables.append(jnp.where(over(codes, sizes.places) == wanted, within(codes, sizes.places) + 1, 0))
    place = jnp.concatenate(tables, axis=0).astype(F32)
    square = (sizes.pieces, sizes.pieces)
    earlier = ones_where(iota(square, 0) < iota(square, 1))
    rank = dot(ones_where(place > 0), earlier)
    shape = (2 * sizes.owners, sizes.slots)
    source = iota(shape, 0)
    source = turn(sizes, over(source, sizes.owners), within(source, sizes.owners))
    offset = iota(shape, 1) - source * sizes.message
    spot = jnp.zeros(shape, F32)
    for each in range(sizes.cap):
        held = jnp.sum(jnp.where(rank == each, place, 0.0), axis=1, keepdims=True)
        spot = jnp.where(offset == each, held, spot)
    return jnp.sum(spot, axis=0, keepdims=True).astype(jnp.int32) - 1


def take_matrix(sizes, places):
    return ones_where(over(iota((sizes.width, sizes.slots), 0), sizes.sub) == places)


def coupled_inverse(sizes, level, limits, inverse, coupling):
    kept = jnp.where(live(limits, level, coupling.shape, 1), coupling, jnp.zeros_like(coupling))
    return dot(kept, inverse).astype(BF16)


def solve_forward(sizes, level, limits, inverse, residual):
    product = dot(inverse, residual)
    return jnp.where(live(limits, level, product.shape, 0), product, 0.0).astype(BF16)


def solve_backward(sizes, level, limits, inverse, side):
    product = trans_dot(inverse, side)
    return jnp.where(live(limits, level, product.shape, 0), product, 0.0)


def fetch(source, target, semaphore):
    copy = pltpu.make_async_copy(source, target, semaphore)
    copy.start()
    return copy


def squared_inverse(sizes, level, limits, inverse):
    kept = jnp.where(live(limits, level, inverse.shape, 0), inverse, jnp.zeros_like(inverse))
    product = trans_dot(inverse, kept)
    return jnp.where(live(limits, level, product.shape, 0), product, 0.0).astype(BF16)


def start_kernel(sizes, right, inverse, coupling, widths, targets, buffer, forward, limits, *refs):
    right_in, targets_in, inverse_in, coupling_in, widths_in, done = refs
    copies = [
        fetch(targets, targets_in, done.at[0]),
        fetch(right.at[0, 0], right_in, done.at[1]),
        fetch(widths.at[0, 0], widths_in, done.at[2]),
        fetch(inverse.at[0, 0, 0], inverse_in, done.at[3]),
        fetch(coupling.at[0, 0, 0], coupling_in, done.at[4]),
    ]
    copies[0].wait()
    sender = send_matrix(sizes, send_slots(sizes, 0, targets_in))
    copies[1].wait()
    residual = repeat_columns(sizes, right_in[0])
    copies[2].wait()
    for level in range(sizes.levels):
        limits[level] = jnp.full((1, LANES), widths_in[level] * BLOCK, jnp.int32)
    copies[3].wait()
    solved = solve_forward(sizes, 0, limits, inverse_in[...], residual)
    forward[...] = solved
    copies[4].wait()
    pieces = keep_own(sizes, dot(coupling_in[...], solved).astype(BF16))
    buffer[...] = dot(sender, pieces).astype(BF16)


def plan_kernel(sizes, inverse, coupling, forward, limits, right, targets, *refs):
    top = sizes.levels - 1
    sends, takes, start, first, last = refs[:5]
    sides, stacks = refs[5 : 5 + top], refs[5 + top : -3]
    inverse_in, coupling_in, done = refs[-3:]
    copies = []
    for level in (*range(1, top + 1), 0):
        at = 2 * len(copies)
        pair = [fetch(inverse.at[0, 0, level], inverse_in.at[level], done.at[at])]
        if level < top:
            pair.append(fetch(coupling.at[0, 0, level], coupling_in.at[level], done.at[at + 1]))
        copies.append(pair)
    for level in range(top):
        sends[level] = send_slots(sizes, level, targets)
        takes[level] = take_places(sizes, level, targets)
    for level in range(1, top + 1):
        sides[level - 1][...] = repeat_columns(sizes, right[level])
    for level in (*range(1, top + 1), 0):
        for copy in copies.pop(0):
            copy.wait()
        block = inverse_in[level]
        if level == top:
            last[...] = squared_inverse(sizes, top, limits, block)
            continue
        product = coupled_inverse(sizes, level, limits, block, coupling_in[level])
        if level == 0:
            first[...] = product
            start[...] = solve_backward(sizes, 0, limits, block, forward[...]).astype(BF16)
        else:
            stacks[level - 1][pl.ds(0, sizes.rows)] = product
            stacks[level - 1][pl.ds(sizes.rows, sizes.width)] = squared_inverse(sizes, level, limits, block)


def residual_of(sizes, level, arrived, side, takes):
    incoming = spread(sizes, dot(take_matrix(sizes, takes[level - 1]), arrived[...]))
    return (side[...].astype(F32) - incoming).astype(BF16)


def up_kernel(sizes, level, arrived, side, stack, sends, takes, buffer, start):
    residual = residual_of(sizes, level, arrived, side, takes)
    both = dot(stack[...], residual)
    pieces = keep_own(sizes, both[: sizes.rows].astype(BF16))
    buffer[...] = dot(send_matrix(sizes, sends[level]), pieces).astype(BF16)
    start[...] = both[sizes.rows :].astype(BF16)


def reply(sizes, level, value, takes):
    return trans_dot(take_matrix(sizes, takes[level - 1]), keep_own(sizes, value)).astype(BF16)


def top_kernel(sizes, level, arrived, side, square, takes, buffer, solved):
    residual = residual_of(sizes, level, arrived, side, takes)
    value = dot(square[...], residual).astype(BF16)
    buffer[...] = reply(sizes, level, value, takes)
    solved[...] = value


def solution_of(sizes, level, arrived, start, product, sends, limits):
    gathered = spread(sizes, trans_dot(send_matrix(sizes, sends[level]), arrived[...])).astype(BF16)
    update = trans_dot(product, gathered)
    update = jnp.where(live(limits, level, update.shape, 0), update, 0.0)
    return (start[...].astype(F32) - update).astype(BF16)


def down_kernel(sizes, level, arrived, start, product, sends, limits, takes, buffer, solved):
    value = solution_of(sizes, level, arrived, start, product[: sizes.rows], sends, limits)
    buffer[...] = reply(sizes, level, value, takes)
    solved[...] = value


def last_kernel(sizes, arrived, start, product, sends, limits, *refs):
    above, out, held, done = refs[:-3], refs[-3], refs[-2], refs[-1]
    count = len(above)
    for level in range(count):
        held[level + 1] = above[level][...].T[: sizes.columns]
    early = fetch(held.at[pl.ds(1, count)], out.at[0, 0, pl.ds(1, count)], done.at[0])
    held[0] = solution_of(sizes, 0, arrived, start, product[...], sends, limits).T[: sizes.columns]
    late = fetch(held.at[0], out.at[0, 0, 0], done.at[1])
    early.wait()
    late.wait()


VMEM = pl.BlockSpec(memory_space=pltpu.VMEM)
HBM = pl.BlockSpec(memory_space=pltpu.HBM)


def call(kernel, name, operands, far, outs, cost, scratch=(), out_spec=VMEM):
    held = [pltpu.with_memory_space_constraint(one, pltpu.HBM) for one in operands[:far]]
    operands = (*held, *operands[far:])
    return pl.pallas_call(
        kernel,
        in_specs=[HBM] * far + [VMEM] * (len(operands) - far),
        out_specs=[out_spec] * len(outs),
        out_shape=[jax.ShapeDtypeStruct(shape, kind) for shape, kind in outs],
        scratch_shapes=scratch,
        compiler_params=pltpu.CompilerParams(vmem_limit_bytes=24 * 2**20),
        cost_estimate=pl.CostEstimate(flops=cost, bytes_accessed=2**20, transcendentals=0),
        name=name,
    )(*operands)


def shards(leaf_axes, right_sides, inverses, couplings, widths, targets):
    right_sides = jnp.swapaxes(right_sides, 3, 4)
    sizes = Sizes(right_sides, couplings, targets, leaf_axes)
    width, slots, rows, columns, levels = sizes.width, sizes.slots, sizes.rows, sizes.columns, sizes.levels
    top = levels - 1
    vector = ((width, LANES), BF16)
    message = ((slots, LANES), BF16)
    matrix = ((width, width), BF16)
    coupled = ((rows, width), BF16)
    stacked = ((rows + width, width), BF16)
    small, large = 10**6, 10**9

    def exchange(buffer, level):
        pair = leaf_axes[len(leaf_axes) - 1 - level % sizes.leaf_bits]
        blocks = buffer.reshape(slots // 2, 2, LANES)
        moved = lax.all_to_all(blocks, ("near", pair, "far"), split_axis=0, concat_axis=0, tiled=True)
        return moved.reshape(slots, LANES)

    inputs = (right_sides, inverses, couplings, widths, targets)
    buffer, *held = call(
        functools.partial(start_kernel, sizes),
        "start",
        inputs,
        5,
        (
            message,
            vector,
            ((levels, 1, LANES), jnp.int32),
            ((levels, columns, width), BF16),
            (targets.shape, jnp.int32),
        ),
        large,
        (
            pltpu.VMEM(*matrix),
            pltpu.VMEM(*coupled),
            pltpu.SMEM((levels,), jnp.int32),
            pltpu.SemaphoreType.DMA((5,)),
        ),
    )
    limits = held[1]
    sends, takes, start, first, last, *planned = call(
        functools.partial(plan_kernel, sizes),
        "plan",
        (inverses, couplings, *held),
        2,
        (
            ((top, 1, rows), jnp.int32),
            ((top, 1, slots), jnp.int32),
            vector,
            coupled,
            matrix,
            *(vector,) * top,
            *(stacked,) * (top - 1),
        ),
        large,
        (
            pltpu.VMEM((levels, width, width), BF16),
            pltpu.VMEM((top, rows, width), BF16),
            pltpu.SemaphoreType.DMA((2 * levels,)),
        ),
    )
    sides, stacks = planned[:top], planned[top:]
    starts = [start]
    for level in range(1, top):
        arrived = exchange(buffer, level - 1)
        buffer, start = call(
            functools.partial(up_kernel, sizes, level),
            f"up_{level}",
            (arrived, sides[level - 1], stacks[level - 1], sends, takes),
            0,
            (message, vector),
            small,
        )
        starts.append(start)
    arrived = exchange(buffer, top - 1)
    buffer, solved = call(
        functools.partial(top_kernel, sizes, top),
        "top",
        (arrived, sides[-1], last, takes),
        0,
        (message, vector),
        small,
    )
    above = [solved]
    for level in reversed(range(1, top)):
        arrived = exchange(buffer, level)
        buffer, solved = call(
            functools.partial(down_kernel, sizes, level),
            f"down_{level}",
            (arrived, starts[level], stacks[level - 1], sends, limits, takes),
            0,
            (message, vector),
            small,
        )
        above.insert(0, solved)
    arrived = exchange(buffer, 0)
    (out,) = call(
        functools.partial(last_kernel, sizes),
        "last",
        (arrived, starts[0], first, sends, limits, *above),
        0,
        ((right_sides.shape, BF16),),
        small,
        (pltpu.VMEM((levels, columns, width), BF16), pltpu.SemaphoreType.DMA((2,))),
        HBM,
    )
    return jnp.swapaxes(out, 3, 4)


def solution(mesh):
    groups, owners = mesh.devices.shape
    bits = groups.bit_length() - 1
    near = 1 if owners % 4 else 4
    leaf_axes = tuple(f"leaf{bit}" for bit in reversed(range(bits)))
    split = Mesh(mesh.devices.reshape((2,) * bits + (owners // near, near)), leaf_axes + ("far", "near"))
    blk = ("far", "near")
    return jax.shard_map(
        functools.partial(shards, leaf_axes),
        mesh=split,
        in_specs=(
            P(leaf_axes, blk, None, None, None),
            P(leaf_axes, blk, None, None, None),
            P(leaf_axes, blk, None, None, None),
            P(leaf_axes, blk, None),
            P(),
        ),
        out_specs=P(leaf_axes, blk, None, None, None),
        check_vma=False,
    )
```

```python
import functools

import jax
import jax.numpy as jnp
from jax import lax
from jax.experimental import pallas as pl
from jax.experimental.pallas import tpu as pltpu
from jax.sharding import Mesh, PartitionSpec as P

BLOCK = 128
LANES = 128
F32 = jnp.float32
BF16 = jnp.bfloat16


def iota(shape, axis):
    return lax.broadcasted_iota(jnp.int32, shape, axis)


def ones_where(condition):
    return jnp.where(condition, 1.0, 0.0).astype(BF16)


def dot(left, right):
    return jnp.dot(left, right, preferred_element_type=F32)


def trans_dot(left, right):
    return lax.dot_general(left, right, (((0,), (0,)), ((), ())), preferred_element_type=F32)


def dot_trans(left, right):
    return lax.dot_general(left, right, (((1,), (1,)), ((), ())), preferred_element_type=F32)


def cross_dot(left, right):
    return lax.dot_general(left, right, (((0,), (1,)), ((), ())), preferred_element_type=F32)


def over(value, size):
    if size & (size - 1):
        return value // size
    return lax.shift_right_logical(value, size.bit_length() - 1)


def within(value, size):
    if size & (size - 1):
        return value % size
    return jnp.bitwise_and(value, size - 1)


class Sizes:
    def __init__(self, right_sides, couplings, targets, leaf_axes):
        self.leaf_axes = leaf_axes
        self.near, self.far = lax.axis_size("near"), lax.axis_size("far")
        self.owners = self.near * self.far
        self.levels, self.columns, self.width = right_sides.shape[-3:]
        self.rows = couplings.shape[-2]
        self.pieces = targets.shape[-1]
        self.leaf_bits = len(leaf_axes)
        self.sub = self.rows // self.pieces
        self.places = self.width // self.sub
        self.cap = max(3, (2 * self.pieces + self.owners - 1) // self.owners + 1)
        self.message = self.cap + self.cap % 2
        self.slots = 2 * self.owners * self.message


def keep_live(limits, level, value, axis):
    return jnp.where(iota(value.shape, axis) < limits[level][:, :1], value, jnp.zeros_like(value))


def keep_own(sizes, value):
    own = within(iota(value.shape, 1), sizes.sub) == over(iota(value.shape, 0), sizes.columns)
    return jnp.where(own, value, jnp.zeros_like(value))


def to_rows(sizes, value):
    value = keep_own(sizes, value)
    parts = [value[at * sizes.columns : (at + 1) * sizes.columns] for at in range(sizes.sub)]
    while len(parts) > 1:
        parts = [sum(parts[at : at + 2]) for at in range(0, len(parts), 2)]
    return parts[0]


def to_flat(sizes, value):
    return keep_own(sizes, jnp.concatenate([value] * sizes.sub, axis=0))


def position(sizes, level):
    group = 0
    for axis in sizes.leaf_axes:
        group = group * 2 + lax.axis_index(axis)
    owner = lax.axis_index("far") * sizes.near + lax.axis_index("near")
    return group, owner, level % sizes.leaf_bits


def turn(sizes, half, owner):
    return (within(owner, sizes.near) * 2 + half) * sizes.far + over(owner, sizes.near)


def send_slots(sizes, level, targets):
    group, owner, bit = position(sizes, level)
    count = sizes.pieces
    table = targets[level, group]
    mine = jnp.sum(jnp.where(iota(table.shape, 0) == owner, table, 0), axis=0, keepdims=True)
    square = (count, count)
    keys_down = jnp.broadcast_to(over(mine, sizes.places), square)
    key_col = jnp.sum(jnp.where(iota(square, 0) == iota(square, 1), keys_down, 0).astype(F32), axis=1, keepdims=True)
    key_col = key_col.astype(jnp.int32)
    earlier = (keys_down == key_col) & (iota(square, 1) < iota(square, 0))
    rank = jnp.sum(jnp.where(earlier, 1.0, 0.0), axis=1, keepdims=True).astype(jnp.int32)
    side, dest = over(key_col, sizes.owners), within(key_col, sizes.owners)
    half = jnp.bitwise_xor(side, lax.shift_right_logical(group, bit) & 1)
    slot = turn(sizes, half, dest) * sizes.message + rank
    shape = (count, sizes.rows)
    chosen = over(iota(shape, 1), sizes.sub) == iota(shape, 0)
    return jnp.sum(jnp.where(chosen, slot, 0).astype(F32), axis=0, keepdims=True).astype(jnp.int32)


def send_matrix(sizes, slots):
    return ones_where(iota((sizes.slots, sizes.rows), 0) == slots)


def take_places(sizes, level, targets):
    group, owner, bit = position(sizes, level)
    own_half = lax.shift_right_logical(group, bit) & 1
    first = group - own_half * 2**bit
    tables = []
    for half in range(2):
        codes = targets[level, first + half * 2**bit]
        wanted = jnp.bitwise_xor(own_half, half) * sizes.owners + owner
        tables.append(jnp.where(over(codes, sizes.places) == wanted, within(codes, sizes.places) + 1, 0))
    place = jnp.concatenate(tables, axis=0).astype(F32)
    square = (sizes.pieces, sizes.pieces)
    earlier = ones_where(iota(square, 0) < iota(square, 1))
    rank = dot(ones_where(place > 0), earlier)
    shape = (2 * sizes.owners, sizes.slots)
    source = iota(shape, 0)
    source = turn(sizes, over(source, sizes.owners), within(source, sizes.owners))
    offset = iota(shape, 1) - source * sizes.message
    spot = jnp.zeros(shape, F32)
    for each in range(sizes.cap):
        held = jnp.sum(jnp.where(rank == each, place, 0.0), axis=1, keepdims=True)
        spot = jnp.where(offset == each, held, spot)
    return jnp.sum(spot, axis=0, keepdims=True).astype(jnp.int32) - 1


def take_matrix(sizes, places):
    return ones_where(over(iota((sizes.width, sizes.slots), 0), sizes.sub) == places)


def coupled_inverse(sizes, level, limits, inverse, coupling):
    return dot(keep_live(limits, level, coupling, 1), inverse).astype(BF16)


def squared_inverse(sizes, level, limits, inverse):
    product = trans_dot(inverse, keep_live(limits, level, inverse, 0))
    return keep_live(limits, level, product, 1).astype(BF16)


def fetch(source, target, semaphore):
    copy = pltpu.make_async_copy(source, target, semaphore)
    copy.start()
    return copy


def send_pieces(sizes, sender, pieces):
    return dot_trans(sender, to_flat(sizes, pieces.astype(BF16))).astype(BF16)


def start_kernel(sizes, right, inverse, coupling, widths, targets, buffer, forward, limits, *refs):
    right_in, targets_in, inverse_in, coupling_in, widths_in, done = refs
    first, others = pl.ds(0, 1), pl.ds(1, sizes.levels - 1)
    copies = [
        fetch(targets.at[first], targets_in.at[first], done.at[0]),
        fetch(right.at[0, 0, first], right_in.at[first], done.at[1]),
        fetch(widths.at[0, 0], widths_in, done.at[2]),
        fetch(inverse.at[0, 0, 0], inverse_in, done.at[3]),
        fetch(coupling.at[0, 0, 0], coupling_in, done.at[4]),
        fetch(right.at[0, 0, others], right_in.at[others], done.at[5]),
        fetch(targets.at[pl.ds(1, sizes.levels - 2)], targets_in.at[pl.ds(1, sizes.levels - 2)], done.at[6]),
    ]
    copies[0].wait()
    sender = send_matrix(sizes, send_slots(sizes, 0, targets_in))
    copies[1].wait()
    copies[2].wait()
    for level in range(sizes.levels):
        limits[level] = jnp.full((1, LANES), widths_in[level] * BLOCK, jnp.int32)
    copies[3].wait()
    solved = keep_live(limits, 0, dot_trans(right_in[0], inverse_in[...]), 1).astype(BF16)
    forward[...] = solved
    copies[4].wait()
    buffer[...] = send_pieces(sizes, sender, dot_trans(solved, coupling_in[...]))
    copies[5].wait()
    copies[6].wait()


def plan_kernel(sizes, inverse, coupling, forward, limits, targets, *refs):
    top = sizes.levels - 1
    sends, takes, start = refs[:3]
    products, squares = refs[3 : 3 + top], refs[3 + top : 3 + 2 * top]
    inverse_in, coupling_in, done = refs[-3:]
    copies = []
    for level in (*range(1, top + 1), 0):
        at = 2 * len(copies)
        pair = [fetch(inverse.at[0, 0, level], inverse_in.at[level], done.at[at])]
        if level < top:
            pair.append(fetch(coupling.at[0, 0, level], coupling_in.at[level], done.at[at + 1]))
        copies.append(pair)
    for level in range(top):
        sends[level] = send_slots(sizes, level, targets)
        takes[level] = take_places(sizes, level, targets)
    for level in (*range(1, top + 1), 0):
        for copy in copies.pop(0):
            copy.wait()
        block = inverse_in[level]
        if level < top:
            products[level][...] = coupled_inverse(sizes, level, limits, block, coupling_in[level])
        if level > 0:
            squares[level - 1][...] = squared_inverse(sizes, level, limits, block)
        else:
            start[...] = keep_live(limits, 0, dot(forward[...], block), 1).astype(BF16)


def residual_of(sizes, level, arrived, right, taker):
    incoming = to_rows(sizes, dot_trans(arrived[...].T, taker))
    return (right[level].astype(F32) - incoming).astype(BF16)


def up_kernel(sizes, level, arrived, right, product, square, sends, takes, buffer, start):
    residual = residual_of(sizes, level, arrived, right, take_matrix(sizes, takes[level - 1]))
    pieces = dot_trans(residual, product[...])
    start[...] = dot(residual, square[...]).astype(BF16)
    buffer[...] = send_pieces(sizes, send_matrix(sizes, sends[level]), pieces)


def top_kernel(sizes, level, arrived, right, square, takes, buffer, solved):
    taker = take_matrix(sizes, takes[level - 1])
    value = dot(residual_of(sizes, level, arrived, right, taker), square[...]).astype(BF16)
    buffer[...] = cross_dot(taker, to_flat(sizes, value)).astype(BF16)
    solved[...] = value


def solution_of(sizes, level, arrived, start, product, sends, limits):
    gathered = to_rows(sizes, dot(arrived[...].T, send_matrix(sizes, sends[level]))).astype(BF16)
    update = keep_live(limits, level, dot(gathered, product[...]), 1)
    return (start[...].astype(F32) - update).astype(BF16)


def down_kernel(sizes, level, arrived, start, product, sends, limits, takes, buffer, solved):
    value = solution_of(sizes, level, arrived, start, product, sends, limits)
    taker = take_matrix(sizes, takes[level - 1])
    buffer[...] = dot(to_flat(sizes, value), taker).astype(BF16).T
    solved[...] = value


def last_kernel(sizes, arrived, start, product, sends, limits, *refs):
    above, out, held, done = refs[:-3], refs[-3], refs[-2], refs[-1]
    copies = [fetch(solved, out.at[0, 0, at + 1], done.at[at + 1]) for at, solved in enumerate(above)]
    held[...] = solution_of(sizes, 0, arrived, start, product, sends, limits)
    copies.append(fetch(held, out.at[0, 0, 0], done.at[0]))
    for copy in copies:
        copy.wait()


VMEM = pl.BlockSpec(memory_space=pltpu.VMEM)
HBM = pl.BlockSpec(memory_space=pltpu.HBM)


def call(kernel, name, operands, far, outs, cost, scratch=(), out_spec=VMEM):
    held = [pltpu.with_memory_space_constraint(one, pltpu.HBM) for one in operands[:far]]
    operands = (*held, *operands[far:])
    return pl.pallas_call(
        kernel,
        in_specs=[HBM] * far + [VMEM] * (len(operands) - far),
        out_specs=[out_spec] * len(outs),
        out_shape=[jax.ShapeDtypeStruct(shape, kind) for shape, kind in outs],
        scratch_shapes=scratch,
        compiler_params=pltpu.CompilerParams(vmem_limit_bytes=24 * 2**20),
        cost_estimate=pl.CostEstimate(flops=cost, bytes_accessed=2**20, transcendentals=0),
        name=name,
    )(*operands)


def shards(leaf_axes, right_sides, inverses, couplings, widths, targets):
    right_sides = jnp.swapaxes(right_sides, 3, 4)
    sizes = Sizes(right_sides, couplings, targets, leaf_axes)
    width, slots, rows, columns, levels = sizes.width, sizes.slots, sizes.rows, sizes.columns, sizes.levels
    top = levels - 1
    vector = ((columns, width), BF16)
    message = ((slots, sizes.sub * columns), BF16)
    matrix = ((width, width), BF16)
    coupled = ((rows, width), BF16)
    small, large = 10**6, 10**9

    def exchange(buffer, level):
        pair = leaf_axes[len(leaf_axes) - 1 - level % sizes.leaf_bits]
        blocks = buffer.reshape(slots // 2, 2, buffer.shape[1])
        moved = lax.all_to_all(blocks, ("near", pair, "far"), split_axis=0, concat_axis=0, tiled=True)
        return moved.reshape(buffer.shape)

    inputs = (right_sides, inverses, couplings, widths, targets)
    buffer, *held = call(
        functools.partial(start_kernel, sizes),
        "start",
        inputs,
        5,
        (
            message,
            vector,
            ((levels, 1, LANES), jnp.int32),
            ((levels, columns, width), BF16),
            (targets.shape, jnp.int32),
        ),
        large,
        (
            pltpu.VMEM(*matrix),
            pltpu.VMEM(*coupled),
            pltpu.SMEM((levels,), jnp.int32),
            pltpu.SemaphoreType.DMA((7,)),
        ),
    )
    forward, limits, right, codes = held
    sends, takes, start, *planned = call(
        functools.partial(plan_kernel, sizes),
        "plan",
        (inverses, couplings, forward, limits, codes),
        2,
        (((top, 1, rows), jnp.int32), ((top, 1, slots), jnp.int32), vector, *(coupled,) * top, *(matrix,) * top),
        large,
        (
            pltpu.VMEM((levels, width, width), BF16),
            pltpu.VMEM((top, rows, width), BF16),
            pltpu.SemaphoreType.DMA((2 * levels,)),
        ),
    )
    products, squares = planned[:top], planned[top:]
    starts = [start]
    for level in range(1, top):
        arrived = exchange(buffer, level - 1)
        buffer, start = call(
            functools.partial(up_kernel, sizes, level),
            f"up_{level}",
            (arrived, right, products[level], squares[level - 1], sends, takes),
            0,
            (message, vector),
            small,
        )
        starts.append(start)
    arrived = exchange(buffer, top - 1)
    buffer, solved = call(
        functools.partial(top_kernel, sizes, top),
        "top",
        (arrived, right, squares[-1], takes),
        0,
        (message, vector),
        small,
    )
    above = [solved]
    for level in reversed(range(1, top)):
        arrived = exchange(buffer, level)
        buffer, solved = call(
            functools.partial(down_kernel, sizes, level),
            f"down_{level}",
            (arrived, starts[level], products[level], sends, limits, takes),
            0,
            (message, vector),
            small,
        )
        above.insert(0, solved)
    arrived = exchange(buffer, 0)
    (out,) = call(
        functools.partial(last_kernel, sizes),
        "last",
        (arrived, starts[0], products[0], sends, limits, *above),
        0,
        ((right_sides.shape, BF16),),
        small,
        (pltpu.VMEM(*vector), pltpu.SemaphoreType.DMA((levels,))),
        HBM,
    )
    return jnp.swapaxes(out, 3, 4)


def solution(mesh):
    groups, owners = mesh.devices.shape
    bits = groups.bit_length() - 1
    near = 1 if owners % 4 else 4
    leaf_axes = tuple(f"leaf{bit}" for bit in reversed(range(bits)))
    split = Mesh(mesh.devices.reshape((2,) * bits + (owners // near, near)), leaf_axes + ("far", "near"))
    blk = ("far", "near")
    return jax.shard_map(
        functools.partial(shards, leaf_axes),
        mesh=split,
        in_specs=(
            P(leaf_axes, blk, None, None, None),
            P(leaf_axes, blk, None, None, None),
            P(leaf_axes, blk, None, None, None),
            P(leaf_axes, blk, None),
            P(),
        ),
        out_specs=P(leaf_axes, blk, None, None, None),
        check_vma=False,
    )
```

```python
import functools

import jax
import jax.numpy as jnp
from jax import lax
from jax.experimental import pallas as pl
from jax.experimental.pallas import tpu as pltpu
from jax.sharding import Mesh, PartitionSpec as P

BLOCK = 128
LANES = 128
F32 = jnp.float32
BF16 = jnp.bfloat16


def iota(shape, axis):
    return lax.broadcasted_iota(jnp.int32, shape, axis)


def ones_where(condition):
    return jnp.where(condition, 1.0, 0.0).astype(BF16)


def dot(left, right):
    return jnp.dot(left, right, preferred_element_type=F32)


def trans_dot(left, right):
    return lax.dot_general(left, right, (((0,), (0,)), ((), ())), preferred_element_type=F32)


def dot_trans(left, right):
    return lax.dot_general(left, right, (((1,), (1,)), ((), ())), preferred_element_type=F32)


def cross_dot(left, right):
    return lax.dot_general(left, right, (((0,), (1,)), ((), ())), preferred_element_type=F32)


def over(value, size):
    if size & (size - 1):
        return value // size
    return lax.shift_right_logical(value, size.bit_length() - 1)


def within(value, size):
    if size & (size - 1):
        return value % size
    return jnp.bitwise_and(value, size - 1)


class Sizes:
    def __init__(self, right_sides, couplings, targets, leaf_axes):
        self.leaf_axes = leaf_axes
        self.near, self.far = lax.axis_size("near"), lax.axis_size("far")
        self.owners = self.near * self.far
        self.levels, self.columns, self.width = right_sides.shape[-3:]
        self.rows = couplings.shape[-2]
        self.pieces = targets.shape[-1]
        self.leaf_bits = len(leaf_axes)
        self.sub = self.rows // self.pieces
        self.places = self.width // self.sub
        self.cap = max(3, (2 * self.pieces + self.owners - 1) // self.owners + 1)
        self.message = self.cap + self.cap % 2
        self.slots = 2 * self.owners * self.message


def keep_live(limits, level, value, axis):
    return jnp.where(iota(value.shape, axis) < limits[level][:, :1], value, jnp.zeros_like(value))


def keep_own(sizes, value):
    own = within(iota(value.shape, 1), sizes.sub) == over(iota(value.shape, 0), sizes.columns)
    return jnp.where(own, value, jnp.zeros_like(value))


def to_rows(sizes, value):
    value = keep_own(sizes, value)
    parts = [value[at * sizes.columns : (at + 1) * sizes.columns] for at in range(sizes.sub)]
    while len(parts) > 1:
        parts = [sum(parts[at : at + 2]) for at in range(0, len(parts), 2)]
    return parts[0]


def to_flat(sizes, value):
    return keep_own(sizes, jnp.concatenate([value] * sizes.sub, axis=0))


def position(sizes, level):
    group = 0
    for axis in sizes.leaf_axes:
        group = group * 2 + lax.axis_index(axis)
    owner = lax.axis_index("far") * sizes.near + lax.axis_index("near")
    return group, owner, level % sizes.leaf_bits


def turn(sizes, half, owner):
    return (within(owner, sizes.near) * 2 + half) * sizes.far + over(owner, sizes.near)


def send_slots(sizes, level, targets):
    group, owner, bit = position(sizes, level)
    count = sizes.pieces
    table = targets[level, group]
    mine = jnp.sum(jnp.where(iota(table.shape, 0) == owner, table, 0), axis=0, keepdims=True)
    square = (count, count)
    keys_down = jnp.broadcast_to(over(mine, sizes.places), square)
    key_col = jnp.sum(jnp.where(iota(square, 0) == iota(square, 1), keys_down, 0).astype(F32), axis=1, keepdims=True)
    key_col = key_col.astype(jnp.int32)
    earlier = (keys_down == key_col) & (iota(square, 1) < iota(square, 0))
    rank = jnp.sum(jnp.where(earlier, 1.0, 0.0), axis=1, keepdims=True).astype(jnp.int32)
    side, dest = over(key_col, sizes.owners), within(key_col, sizes.owners)
    half = jnp.bitwise_xor(side, lax.shift_right_logical(group, bit) & 1)
    slot = turn(sizes, half, dest) * sizes.message + rank
    shape = (count, sizes.rows)
    chosen = over(iota(shape, 1), sizes.sub) == iota(shape, 0)
    return jnp.sum(jnp.where(chosen, slot, 0).astype(F32), axis=0, keepdims=True).astype(jnp.int32)


def send_matrix(sizes, slots):
    return ones_where(iota((sizes.slots, sizes.rows), 0) == slots)


def take_places(sizes, level, targets):
    group, owner, bit = position(sizes, level)
    own_half = lax.shift_right_logical(group, bit) & 1
    first = group - own_half * 2**bit
    tables = []
    for half in range(2):
        codes = targets[level, first + half * 2**bit]
        wanted = jnp.bitwise_xor(own_half, half) * sizes.owners + owner
        tables.append(jnp.where(over(codes, sizes.places) == wanted, within(codes, sizes.places) + 1, 0))
    place = jnp.concatenate(tables, axis=0).astype(F32)
    square = (sizes.pieces, sizes.pieces)
    earlier = ones_where(iota(square, 0) < iota(square, 1))
    rank = dot(ones_where(place > 0), earlier)
    shape = (2 * sizes.owners, sizes.slots)
    source = iota(shape, 0)
    source = turn(sizes, over(source, sizes.owners), within(source, sizes.owners))
    offset = iota(shape, 1) - source * sizes.message
    spot = jnp.zeros(shape, F32)
    for each in range(sizes.cap):
        held = jnp.sum(jnp.where(rank == each, place, 0.0), axis=1, keepdims=True)
        spot = jnp.where(offset == each, held, spot)
    return jnp.sum(spot, axis=0, keepdims=True).astype(jnp.int32) - 1


def take_matrix(sizes, places):
    return ones_where(over(iota((sizes.width, sizes.slots), 0), sizes.sub) == places)


def coupled_inverse(sizes, level, limits, inverse, coupling):
    return dot(keep_live(limits, level, coupling, 1), inverse).astype(BF16)


def squared_inverse(sizes, level, limits, inverse):
    product = trans_dot(inverse, keep_live(limits, level, inverse, 0))
    return keep_live(limits, level, product, 1).astype(BF16)


def solve_forward(sizes, level, limits, residual, inverse):
    return keep_live(limits, level, dot_trans(residual, inverse[...]), 1).astype(BF16)


def solve_back(sizes, level, limits, solved, inverse):
    return keep_live(limits, level, dot(solved, inverse[...]), 1).astype(BF16)


def fetch(source, target, semaphore):
    copy = pltpu.make_async_copy(source, target, semaphore)
    copy.start()
    return copy


def send_pieces(sizes, sender, pieces):
    return dot_trans(sender, to_flat(sizes, pieces.astype(BF16))).astype(BF16)


def start_kernel(sizes, right, inverse, coupling, widths, targets, buffer, forward, limits, *refs):
    right_in, targets_in, inverse_in, coupling_in, widths_in, done = refs
    first, others = pl.ds(0, 1), pl.ds(1, sizes.levels - 1)
    copies = [
        fetch(targets.at[first], targets_in.at[first], done.at[0]),
        fetch(right.at[0, 0, first], right_in.at[first], done.at[1]),
        fetch(widths.at[0, 0], widths_in, done.at[2]),
        fetch(inverse.at[0, 0, 0], inverse_in, done.at[3]),
        fetch(coupling.at[0, 0, 0], coupling_in, done.at[4]),
        fetch(right.at[0, 0, others], right_in.at[others], done.at[5]),
        fetch(targets.at[pl.ds(1, sizes.levels - 2)], targets_in.at[pl.ds(1, sizes.levels - 2)], done.at[6]),
    ]
    copies[0].wait()
    sender = send_matrix(sizes, send_slots(sizes, 0, targets_in))
    copies[1].wait()
    copies[2].wait()
    for level in range(sizes.levels):
        limits[level] = jnp.full((1, LANES), widths_in[level] * BLOCK, jnp.int32)
    copies[3].wait()
    solved = solve_forward(sizes, 0, limits, right_in[0], inverse_in)
    forward[...] = solved
    copies[4].wait()
    buffer[...] = send_pieces(sizes, sender, dot_trans(solved, coupling_in[...]))
    copies[5].wait()
    copies[6].wait()


def plan_kernel(sizes, inverse, coupling, forward, limits, targets, *refs):
    top = sizes.levels - 1
    sends, takes, start = refs[:3]
    products, blocks, square = refs[3 : 3 + top], refs[3 + top : 2 + 2 * top], refs[2 + 2 * top]
    first_in, top_in, coupling_in, done = refs[-4:]
    held = (first_in, *blocks, top_in)
    copies = []
    for level in (*range(1, top + 1), 0):
        at = 2 * len(copies)
        pair = [fetch(inverse.at[0, 0, level], held[level], done.at[at])]
        if level < top:
            pair.append(fetch(coupling.at[0, 0, level], coupling_in.at[level], done.at[at + 1]))
        copies.append(pair)
    for level in range(top):
        sends[level] = send_slots(sizes, level, targets)
        takes[level] = take_places(sizes, level, targets)
    for level in (*range(1, top + 1), 0):
        for copy in copies.pop(0):
            copy.wait()
        block = held[level][...]
        if level < top:
            products[level][...] = coupled_inverse(sizes, level, limits, block, coupling_in[level])
        else:
            square[...] = squared_inverse(sizes, level, limits, block)
    start[...] = solve_back(sizes, 0, limits, forward[...], first_in)


def residual_of(sizes, level, arrived, right, taker):
    incoming = to_rows(sizes, dot_trans(arrived[...].T, taker))
    return (right[level].astype(F32) - incoming).astype(BF16)


def up_kernel(sizes, level, arrived, right, product, inverse, sends, limits, takes, buffer, start):
    residual = residual_of(sizes, level, arrived, right, take_matrix(sizes, takes[level - 1]))
    pieces = dot_trans(residual, product[...])
    solved = solve_forward(sizes, level, limits, residual, inverse)
    buffer[...] = send_pieces(sizes, send_matrix(sizes, sends[level]), pieces)
    start[...] = solve_back(sizes, level, limits, solved, inverse)


def top_kernel(sizes, level, arrived, right, square, takes, buffer, solved):
    taker = take_matrix(sizes, takes[level - 1])
    value = dot(residual_of(sizes, level, arrived, right, taker), square[...]).astype(BF16)
    buffer[...] = cross_dot(taker, to_flat(sizes, value)).astype(BF16)
    solved[...] = value


def solution_of(sizes, level, arrived, start, product, sends, limits):
    gathered = to_rows(sizes, dot(arrived[...].T, send_matrix(sizes, sends[level]))).astype(BF16)
    update = keep_live(limits, level, dot(gathered, product[...]), 1)
    return (start[...].astype(F32) - update).astype(BF16)


def down_kernel(sizes, level, arrived, start, product, sends, limits, takes, buffer, solved):
    value = solution_of(sizes, level, arrived, start, product, sends, limits)
    taker = take_matrix(sizes, takes[level - 1])
    buffer[...] = dot(to_flat(sizes, value), taker).astype(BF16).T
    solved[...] = value


def last_kernel(sizes, arrived, start, product, sends, limits, *refs):
    above, out, held, done = refs[:-3], refs[-3], refs[-2], refs[-1]
    copies = [fetch(solved, out.at[0, 0, at + 1], done.at[at + 1]) for at, solved in enumerate(above)]
    held[...] = solution_of(sizes, 0, arrived, start, product, sends, limits)
    copies.append(fetch(held, out.at[0, 0, 0], done.at[0]))
    for copy in copies:
        copy.wait()


VMEM = pl.BlockSpec(memory_space=pltpu.VMEM)
HBM = pl.BlockSpec(memory_space=pltpu.HBM)


def call(kernel, name, operands, far, outs, cost, scratch=(), out_spec=VMEM):
    held = [pltpu.with_memory_space_constraint(one, pltpu.HBM) for one in operands[:far]]
    operands = (*held, *operands[far:])
    return pl.pallas_call(
        kernel,
        in_specs=[HBM] * far + [VMEM] * (len(operands) - far),
        out_specs=[out_spec] * len(outs),
        out_shape=[jax.ShapeDtypeStruct(shape, kind) for shape, kind in outs],
        scratch_shapes=scratch,
        compiler_params=pltpu.CompilerParams(vmem_limit_bytes=24 * 2**20),
        cost_estimate=pl.CostEstimate(flops=cost, bytes_accessed=2**20, transcendentals=0),
        name=name,
    )(*operands)


def shards(leaf_axes, right_sides, inverses, couplings, widths, targets):
    right_sides = jnp.swapaxes(right_sides, 3, 4)
    sizes = Sizes(right_sides, couplings, targets, leaf_axes)
    width, slots, rows, columns, levels = sizes.width, sizes.slots, sizes.rows, sizes.columns, sizes.levels
    top = levels - 1
    vector = ((columns, width), BF16)
    message = ((slots, sizes.sub * columns), BF16)
    matrix = ((width, width), BF16)
    coupled = ((rows, width), BF16)
    small, large = 10**6, 10**9

    def exchange(buffer, level):
        pair = leaf_axes[len(leaf_axes) - 1 - level % sizes.leaf_bits]
        blocks = buffer.reshape(slots // 2, 2, buffer.shape[1])
        moved = lax.all_to_all(blocks, ("near", pair, "far"), split_axis=0, concat_axis=0, tiled=True)
        return moved.reshape(buffer.shape)

    inputs = (right_sides, inverses, couplings, widths, targets)
    buffer, *held = call(
        functools.partial(start_kernel, sizes),
        "start",
        inputs,
        5,
        (
            message,
            vector,
            ((levels, 1, LANES), jnp.int32),
            ((levels, columns, width), BF16),
            (targets.shape, jnp.int32),
        ),
        large,
        (
            pltpu.VMEM(*matrix),
            pltpu.VMEM(*coupled),
            pltpu.SMEM((levels,), jnp.int32),
            pltpu.SemaphoreType.DMA((7,)),
        ),
    )
    forward, limits, right, codes = held
    sends, takes, start, *planned = call(
        functools.partial(plan_kernel, sizes),
        "plan",
        (inverses, couplings, forward, limits, codes),
        2,
        (((top, 1, rows), jnp.int32), ((top, 1, slots), jnp.int32), vector, *(coupled,) * top, *(matrix,) * top),
        large,
        (
            pltpu.VMEM(*matrix),
            pltpu.VMEM(*matrix),
            pltpu.VMEM((top, rows, width), BF16),
            pltpu.SemaphoreType.DMA((2 * levels,)),
        ),
    )
    products, blocks = planned[:top], planned[top:]
    starts = [start]
    for level in range(1, top):
        arrived = exchange(buffer, level - 1)
        buffer, start = call(
            functools.partial(up_kernel, sizes, level),
            f"up_{level}",
            (arrived, right, products[level], blocks[level - 1], sends, limits, takes),
            0,
            (message, vector),
            small,
        )
        starts.append(start)
    arrived = exchange(buffer, top - 1)
    buffer, solved = call(
        functools.partial(top_kernel, sizes, top),
        "top",
        (arrived, right, blocks[-1], takes),
        0,
        (message, vector),
        small,
    )
    above = [solved]
    for level in reversed(range(1, top)):
        arrived = exchange(buffer, level)
        buffer, solved = call(
            functools.partial(down_kernel, sizes, level),
            f"down_{level}",
            (arrived, starts[level], products[level], sends, limits, takes),
            0,
            (message, vector),
            small,
        )
        above.insert(0, solved)
    arrived = exchange(buffer, 0)
    (out,) = call(
        functools.partial(last_kernel, sizes),
        "last",
        (arrived, starts[0], products[0], sends, limits, *above),
        0,
        ((right_sides.shape, BF16),),
        small,
        (pltpu.VMEM(*vector), pltpu.SemaphoreType.DMA((levels,))),
        HBM,
    )
    return jnp.swapaxes(out, 3, 4)


def solution(mesh):
    groups, owners = mesh.devices.shape
    bits = groups.bit_length() - 1
    near = 1 if owners % 4 else 4
    leaf_axes = tuple(f"leaf{bit}" for bit in reversed(range(bits)))
    split = Mesh(mesh.devices.reshape((2,) * bits + (owners // near, near)), leaf_axes + ("far", "near"))
    blk = ("far", "near")
    return jax.shard_map(
        functools.partial(shards, leaf_axes),
        mesh=split,
        in_specs=(
            P(leaf_axes, blk, None, None, None),
            P(leaf_axes, blk, None, None, None),
            P(leaf_axes, blk, None, None, None),
            P(leaf_axes, blk, None),
            P(),
        ),
        out_specs=P(leaf_axes, blk, None, None, None),
        check_vma=False,
    )
```

```python
import functools

import jax
import jax.numpy as jnp
from jax import lax
from jax.experimental import pallas as pl
from jax.experimental.pallas import tpu as pltpu
from jax.sharding import Mesh, PartitionSpec as P

BLOCK = 128
LANES = 128
F32 = jnp.float32
BF16 = jnp.bfloat16


def iota(shape, axis):
    return lax.broadcasted_iota(jnp.int32, shape, axis)


def ones_where(condition):
    return jnp.where(condition, 1.0, 0.0).astype(BF16)


def dot(left, right):
    return jnp.dot(left, right, preferred_element_type=F32)


def trans_dot(left, right):
    return lax.dot_general(left, right, (((0,), (0,)), ((), ())), preferred_element_type=F32)


def dot_trans(left, right):
    return lax.dot_general(left, right, (((1,), (1,)), ((), ())), preferred_element_type=F32)


def cross_dot(left, right):
    return lax.dot_general(left, right, (((0,), (1,)), ((), ())), preferred_element_type=F32)


def over(value, size):
    if size & (size - 1):
        return value // size
    return lax.shift_right_logical(value, size.bit_length() - 1)


def within(value, size):
    if size & (size - 1):
        return value % size
    return jnp.bitwise_and(value, size - 1)


class Sizes:
    def __init__(self, right_sides, couplings, targets, leaf_axes):
        self.leaf_axes = leaf_axes
        self.near, self.far = lax.axis_size("near"), lax.axis_size("far")
        self.owners = self.near * self.far
        self.levels, self.columns, self.width = right_sides.shape[-3:]
        self.rows = couplings.shape[-2]
        self.pieces = targets.shape[-1]
        self.leaf_bits = len(leaf_axes)
        self.sub = self.rows // self.pieces
        self.places = self.width // self.sub
        self.cap = max(3, (2 * self.pieces + self.owners - 1) // self.owners + 1)
        self.message = self.cap + self.cap % 2
        self.slots = 2 * self.owners * self.message


def keep_live(limits, level, value, axis):
    return jnp.where(iota(value.shape, axis) < limits[level][:, :1], value, jnp.zeros_like(value))


def keep_own(sizes, value):
    own = within(iota(value.shape, 1), sizes.sub) == over(iota(value.shape, 0), sizes.columns)
    return jnp.where(own, value, jnp.zeros_like(value))


def to_rows(sizes, value):
    value = keep_own(sizes, value)
    parts = [value[at * sizes.columns : (at + 1) * sizes.columns] for at in range(sizes.sub)]
    while len(parts) > 1:
        parts = [sum(parts[at : at + 2]) for at in range(0, len(parts), 2)]
    return parts[0]


def to_flat(sizes, value):
    return keep_own(sizes, jnp.concatenate([value] * sizes.sub, axis=0))


def position(sizes, level):
    group = 0
    for axis in sizes.leaf_axes:
        group = group * 2 + lax.axis_index(axis)
    owner = lax.axis_index("far") * sizes.near + lax.axis_index("near")
    return group, owner, level % sizes.leaf_bits


def turn(sizes, half, owner):
    return (within(owner, sizes.near) * 2 + half) * sizes.far + over(owner, sizes.near)


def send_slots(sizes, level, targets):
    group, owner, bit = position(sizes, level)
    count = sizes.pieces
    table = targets[level, group]
    mine = jnp.sum(jnp.where(iota(table.shape, 0) == owner, table, 0), axis=0, keepdims=True)
    square = (count, count)
    keys_down = jnp.broadcast_to(over(mine, sizes.places), square)
    key_col = jnp.sum(jnp.where(iota(square, 0) == iota(square, 1), keys_down, 0).astype(F32), axis=1, keepdims=True)
    key_col = key_col.astype(jnp.int32)
    earlier = (keys_down == key_col) & (iota(square, 1) < iota(square, 0))
    rank = jnp.sum(jnp.where(earlier, 1.0, 0.0), axis=1, keepdims=True).astype(jnp.int32)
    side, dest = over(key_col, sizes.owners), within(key_col, sizes.owners)
    half = jnp.bitwise_xor(side, lax.shift_right_logical(group, bit) & 1)
    slot = turn(sizes, half, dest) * sizes.message + rank
    shape = (count, sizes.rows)
    chosen = over(iota(shape, 1), sizes.sub) == iota(shape, 0)
    return jnp.sum(jnp.where(chosen, slot, 0).astype(F32), axis=0, keepdims=True).astype(jnp.int32)


def send_matrix(sizes, slots):
    return ones_where(iota((sizes.slots, sizes.rows), 0) == slots)


def take_places(sizes, level, targets):
    group, owner, bit = position(sizes, level)
    own_half = lax.shift_right_logical(group, bit) & 1
    first = group - own_half * 2**bit
    tables = []
    for half in range(2):
        codes = targets[level, first + half * 2**bit]
        wanted = jnp.bitwise_xor(own_half, half) * sizes.owners + owner
        tables.append(jnp.where(over(codes, sizes.places) == wanted, within(codes, sizes.places) + 1, 0))
    place = jnp.concatenate(tables, axis=0).astype(F32)
    square = (sizes.pieces, sizes.pieces)
    earlier = ones_where(iota(square, 0) < iota(square, 1))
    rank = dot(ones_where(place > 0), earlier)
    shape = (2 * sizes.owners, sizes.slots)
    source = iota(shape, 0)
    source = turn(sizes, over(source, sizes.owners), within(source, sizes.owners))
    offset = iota(shape, 1) - source * sizes.message
    spot = jnp.zeros(shape, F32)
    for each in range(sizes.cap):
        held = jnp.sum(jnp.where(rank == each, place, 0.0), axis=1, keepdims=True)
        spot = jnp.where(offset == each, held, spot)
    return jnp.sum(spot, axis=0, keepdims=True).astype(jnp.int32) - 1


def take_matrix(sizes, places):
    return ones_where(over(iota((sizes.width, sizes.slots), 0), sizes.sub) == places)


def coupled_inverse(sizes, level, limits, inverse, coupling):
    return dot(keep_live(limits, level, coupling, 1), inverse).astype(BF16)


def squared_inverse(sizes, level, limits, inverse):
    product = trans_dot(inverse, keep_live(limits, level, inverse, 0))
    return keep_live(limits, level, product, 1).astype(BF16)


def solve_forward(sizes, level, limits, residual, inverse):
    return keep_live(limits, level, dot_trans(residual, inverse[...]), 1).astype(BF16)


def solve_back(sizes, level, limits, solved, inverse):
    return keep_live(limits, level, dot(solved, inverse[...]), 1).astype(BF16)


def fetch(source, target, semaphore):
    copy = pltpu.make_async_copy(source, target, semaphore)
    copy.start()
    return copy


def send_pieces(sizes, sender, pieces):
    return dot_trans(sender, to_flat(sizes, pieces.astype(BF16))).astype(BF16)


def start_kernel(sizes, right, inverse, coupling, widths, targets, buffer, forward, limits, *refs):
    right_in, targets_in, send, next_send, next_take, product = refs[:6]
    held, below, widths_in, done = refs[6:-3], refs[-3], refs[-2], refs[-1]
    held = (*held[:3], below, *held[3:])
    copies = [
        fetch(targets, targets_in, done.at[0]),
        fetch(right.at[0, 0], right_in, done.at[1]),
        fetch(widths.at[0, 0], widths_in, done.at[2]),
    ]
    for at, target in enumerate(held):
        copies.append(fetch((inverse, coupling)[at % 2].at[0, 0, at // 2], target, done.at[3 + at]))
    copies[0].wait()
    slots = send_slots(sizes, 0, targets_in)
    send[...] = slots
    sender = send_matrix(sizes, slots)
    copies[1].wait()
    copies[2].wait()
    for level in range(sizes.levels):
        limits[level] = jnp.full((1, LANES), widths_in[level] * BLOCK, jnp.int32)
    for copy in copies[3:5]:
        copy.wait()
    next_send[...] = send_slots(sizes, 1, targets_in)
    next_take[...] = take_places(sizes, 0, targets_in)
    solved = solve_forward(sizes, 0, limits, right_in[0], held[0])
    forward[...] = solved
    pieces = dot_trans(solved, held[1][...])
    for copy in copies[5:7]:
        copy.wait()
    product[...] = coupled_inverse(sizes, 1, limits, held[2][...], held[3][...])
    buffer[...] = send_pieces(sizes, sender, pieces)
    for copy in copies[7:]:
        copy.wait()


def residual_of(sizes, level, arrived, right, taker):
    incoming = to_rows(sizes, dot_trans(arrived[...].T, taker))
    return (right[level].astype(F32) - incoming).astype(BF16)


def up_kernel(sizes, level, arrived, right, limits, targets, product, inverse, send, take, *refs):
    block, below, buffer, start, next_take, next_product, *more = refs
    next_take[...] = take_places(sizes, level, targets)
    following = (level + 1) % (sizes.levels - 1)
    if following:
        more[0][...] = send_slots(sizes, following, targets)
    residual = residual_of(sizes, level, arrived, right, take_matrix(sizes, take[...]))
    pieces = dot_trans(residual, product[...])
    next_product[...] = coupled_inverse(sizes, following, limits, block[...], below[...])
    solved = solve_forward(sizes, level, limits, residual, inverse)
    buffer[...] = send_pieces(sizes, send_matrix(sizes, send[...]), pieces)
    start[...] = solve_back(sizes, level, limits, solved, inverse)


def top_kernel(sizes, level, arrived, right, limits, inverse, take, forward, first, buffer, solution, start):
    taker = take_matrix(sizes, take[...])
    solved = solve_forward(sizes, level, limits, residual_of(sizes, level, arrived, right, taker), inverse)
    start[...] = solve_back(sizes, 0, limits, forward[...], first)
    value = solve_back(sizes, level, limits, solved, inverse)
    buffer[...] = cross_dot(taker, to_flat(sizes, value)).astype(BF16)
    solution[...] = value


def solution_of(sizes, level, arrived, start, product, send, limits):
    gathered = to_rows(sizes, dot(arrived[...].T, send_matrix(sizes, send[...]))).astype(BF16)
    update = keep_live(limits, level, dot(gathered, product[...]), 1)
    return (start[...].astype(F32) - update).astype(BF16)


def down_kernel(sizes, level, arrived, start, product, send, limits, take, buffer, solved):
    value = solution_of(sizes, level, arrived, start, product, send, limits)
    buffer[...] = dot(to_flat(sizes, value), take_matrix(sizes, take[...])).astype(BF16).T
    solved[...] = value


def last_kernel(sizes, arrived, start, product, send, limits, *refs):
    above, out, held, done = refs[:-3], refs[-3], refs[-2], refs[-1]
    copies = [fetch(solved, out.at[0, 0, at + 1], done.at[at + 1]) for at, solved in enumerate(above)]
    held[...] = solution_of(sizes, 0, arrived, start, product, send, limits)
    copies.append(fetch(held, out.at[0, 0, 0], done.at[0]))
    for copy in copies:
        copy.wait()


VMEM = pl.BlockSpec(memory_space=pltpu.VMEM)
HBM = pl.BlockSpec(memory_space=pltpu.HBM)


def call(kernel, name, operands, far, outs, cost, scratch=(), out_spec=VMEM):
    held = [pltpu.with_memory_space_constraint(one, pltpu.HBM) for one in operands[:far]]
    operands = (*held, *operands[far:])
    return pl.pallas_call(
        kernel,
        in_specs=[HBM] * far + [VMEM] * (len(operands) - far),
        out_specs=[out_spec] * len(outs),
        out_shape=[jax.ShapeDtypeStruct(shape, kind) for shape, kind in outs],
        scratch_shapes=scratch,
        compiler_params=pltpu.CompilerParams(vmem_limit_bytes=24 * 2**20),
        cost_estimate=pl.CostEstimate(flops=cost, bytes_accessed=2**20, transcendentals=0),
        name=name,
    )(*operands)


def shards(leaf_axes, right_sides, inverses, couplings, widths, targets):
    right_sides = jnp.swapaxes(right_sides, 3, 4)
    sizes = Sizes(right_sides, couplings, targets, leaf_axes)
    width, slots, rows, columns, levels = sizes.width, sizes.slots, sizes.rows, sizes.columns, sizes.levels
    top = levels - 1
    vector = ((columns, width), BF16)
    message = ((slots, sizes.sub * columns), BF16)
    matrix = ((width, width), BF16)
    coupled = ((rows, width), BF16)
    send_row, take_row = ((1, rows), jnp.int32), ((1, slots), jnp.int32)
    small, large = 10**6, 10**9

    def exchange(buffer, level):
        pair = leaf_axes[len(leaf_axes) - 1 - level % sizes.leaf_bits]
        blocks = buffer.reshape(slots // 2, 2, buffer.shape[1])
        moved = lax.all_to_all(blocks, ("near", pair, "far"), split_axis=0, concat_axis=0, tiled=True)
        return moved.reshape(buffer.shape)

    inputs = (right_sides, inverses, couplings, widths, targets)
    buffer, forward, limits, right, codes, send, next_send, take, product, *held = call(
        functools.partial(start_kernel, sizes),
        "start",
        inputs,
        5,
        (
            message,
            vector,
            ((levels, 1, LANES), jnp.int32),
            ((levels, columns, width), BF16),
            (targets.shape, jnp.int32),
            send_row,
            send_row,
            take_row,
            coupled,
            matrix,
            coupled,
            matrix,
            *(matrix, coupled) * (top - 2),
            matrix,
        ),
        large,
        (pltpu.VMEM(*coupled), pltpu.SMEM((levels,), jnp.int32), pltpu.SemaphoreType.DMA((4 + 2 * top,))),
    )
    held.insert(3, None)
    blocks, below = held[::2], held[1::2]
    sends, takes, products, starts = [send, next_send], [take], [None, product], [None]
    for level in range(1, top):
        arrived = exchange(buffer, level - 1)
        following = (level + 1) % top
        buffer, start, take, product, *more = call(
            functools.partial(up_kernel, sizes, level),
            f"up_{level}",
            (arrived, right, limits, codes, products[level], blocks[level], sends[level], takes[-1], blocks[following], below[following]),
            0,
            (message, vector, take_row, coupled, *((send_row,) if following else ())),
            small,
        )
        starts.append(start)
        takes.append(take)
        sends.extend(more)
        products.append(product)
    arrived = exchange(buffer, top - 1)
    products[0] = products.pop()
    buffer, solved, starts[0] = call(
        functools.partial(top_kernel, sizes, top),
        "top",
        (arrived, right, limits, blocks[top], takes[-1], forward, blocks[0]),
        0,
        (message, vector, vector),
        small,
    )
    above = [solved]
    for level in reversed(range(1, top)):
        arrived = exchange(buffer, level)
        buffer, solved = call(
            functools.partial(down_kernel, sizes, level),
            f"down_{level}",
            (arrived, starts[level], products[level], sends[level], limits, takes[level - 1]),
            0,
            (message, vector),
            small,
        )
        above.insert(0, solved)
    arrived = exchange(buffer, 0)
    (out,) = call(
        functools.partial(last_kernel, sizes),
        "last",
        (arrived, starts[0], products[0], sends[0], limits, *above),
        0,
        ((right_sides.shape, BF16),),
        small,
        (pltpu.VMEM(*vector), pltpu.SemaphoreType.DMA((levels,))),
        HBM,
    )
    return jnp.swapaxes(out, 3, 4)


def solution(mesh):
    groups, owners = mesh.devices.shape
    bits = groups.bit_length() - 1
    near = 1 if owners % 4 else 4
    leaf_axes = tuple(f"leaf{bit}" for bit in reversed(range(bits)))
    split = Mesh(mesh.devices.reshape((2,) * bits + (owners // near, near)), leaf_axes + ("far", "near"))
    blk = ("far", "near")
    return jax.shard_map(
        functools.partial(shards, leaf_axes),
        mesh=split,
        in_specs=(
            P(leaf_axes, blk, None, None, None),
            P(leaf_axes, blk, None, None, None),
            P(leaf_axes, blk, None, None, None),
            P(leaf_axes, blk, None),
            P(),
        ),
        out_specs=P(leaf_axes, blk, None, None, None),
        check_vma=False,
    )
```

```python
import functools

import jax
import jax.numpy as jnp
from jax import lax
from jax.experimental import pallas as pl
from jax.experimental.pallas import tpu as pltpu
from jax.sharding import Mesh, PartitionSpec as P

BLOCK = 128
LANES = 128
F32 = jnp.float32
BF16 = jnp.bfloat16


def iota(shape, axis):
    return lax.broadcasted_iota(jnp.int32, shape, axis)


def ones_where(condition):
    return jnp.where(condition, 1.0, 0.0).astype(BF16)


def dot(left, right):
    return jnp.dot(left, right, preferred_element_type=F32)


def trans_dot(left, right):
    return lax.dot_general(left, right, (((0,), (0,)), ((), ())), preferred_element_type=F32)


def dot_trans(left, right):
    return lax.dot_general(left, right, (((1,), (1,)), ((), ())), preferred_element_type=F32)


def cross_dot(left, right):
    return lax.dot_general(left, right, (((0,), (1,)), ((), ())), preferred_element_type=F32)


def over(value, size):
    if size & (size - 1):
        return value // size
    return lax.shift_right_logical(value, size.bit_length() - 1)


def within(value, size):
    if size & (size - 1):
        return value % size
    return jnp.bitwise_and(value, size - 1)


class Sizes:
    def __init__(self, right_sides, couplings, targets, leaf_axes):
        self.leaf_axes = leaf_axes
        self.near, self.far = lax.axis_size("near"), lax.axis_size("far")
        self.owners = self.near * self.far
        self.levels, self.columns, self.width = right_sides.shape[-3:]
        self.rows = couplings.shape[-2]
        self.pieces = targets.shape[-1]
        self.leaf_bits = len(leaf_axes)
        self.sub = self.rows // self.pieces
        self.places = self.width // self.sub
        self.cap = max(3, (2 * self.pieces + self.owners - 1) // self.owners + 1)
        self.message = self.cap + self.cap % 2
        self.slots = 2 * self.owners * self.message


def keep_live(limits, level, value, axis):
    return jnp.where(iota(value.shape, axis) < limits[level][:, :1], value, jnp.zeros_like(value))


def keep_own(sizes, value):
    own = within(iota(value.shape, 1), sizes.sub) == over(iota(value.shape, 0), sizes.columns)
    return jnp.where(own, value, jnp.zeros_like(value))


def to_rows(sizes, value):
    value = keep_own(sizes, value)
    parts = [value[at * sizes.columns : (at + 1) * sizes.columns] for at in range(sizes.sub)]
    while len(parts) > 1:
        parts = [sum(parts[at : at + 2]) for at in range(0, len(parts), 2)]
    return parts[0]


def to_flat(sizes, value):
    return keep_own(sizes, jnp.concatenate([value] * sizes.sub, axis=0))


def position(sizes, level):
    group = 0
    for axis in sizes.leaf_axes:
        group = group * 2 + lax.axis_index(axis)
    owner = lax.axis_index("far") * sizes.near + lax.axis_index("near")
    return group, owner, level % sizes.leaf_bits


def turn(sizes, half, owner):
    at = (within(owner, sizes.near) * 2 + half) * sizes.far + over(owner, sizes.near)
    shift = 1
    while shift < 2 * sizes.owners:
        at = jnp.bitwise_xor(at, lax.shift_right_logical(at, shift))
        shift *= 2
    return at


def turns(sizes, bit):
    low = 2**bit
    order = []
    for group in range(2 ** sizes.leaf_bits):
        if group & low:
            continue
        members = []
        for at in range(2 * sizes.owners):
            at ^= at >> 1
            near, half, far = at // (2 * sizes.far), at // sizes.far % 2, at % sizes.far
            members.append((group + half * low) * sizes.owners + far * sizes.near + near)
        order.append(members)
    return order


def send_slots(sizes, level, targets):
    group, owner, bit = position(sizes, level)
    count = sizes.pieces
    table = targets[level, group]
    mine = jnp.sum(jnp.where(iota(table.shape, 0) == owner, table, 0), axis=0, keepdims=True)
    square = (count, count)
    keys_down = jnp.broadcast_to(over(mine, sizes.places), square)
    key_col = jnp.sum(jnp.where(iota(square, 0) == iota(square, 1), keys_down, 0).astype(F32), axis=1, keepdims=True)
    key_col = key_col.astype(jnp.int32)
    earlier = (keys_down == key_col) & (iota(square, 1) < iota(square, 0))
    rank = jnp.sum(jnp.where(earlier, 1.0, 0.0), axis=1, keepdims=True).astype(jnp.int32)
    side, dest = over(key_col, sizes.owners), within(key_col, sizes.owners)
    half = jnp.bitwise_xor(side, lax.shift_right_logical(group, bit) & 1)
    slot = turn(sizes, half, dest) * sizes.message + rank
    shape = (count, sizes.rows)
    chosen = over(iota(shape, 1), sizes.sub) == iota(shape, 0)
    return jnp.sum(jnp.where(chosen, slot, 0).astype(F32), axis=0, keepdims=True).astype(jnp.int32)


def send_matrix(sizes, slots):
    return ones_where(iota((sizes.slots, sizes.rows), 0) == slots)


def take_places(sizes, level, targets):
    group, owner, bit = position(sizes, level)
    own_half = lax.shift_right_logical(group, bit) & 1
    first = group - own_half * 2**bit
    tables = []
    for half in range(2):
        codes = targets[level, first + half * 2**bit]
        wanted = jnp.bitwise_xor(own_half, half) * sizes.owners + owner
        tables.append(jnp.where(over(codes, sizes.places) == wanted, within(codes, sizes.places) + 1, 0))
    place = jnp.concatenate(tables, axis=0).astype(F32)
    square = (sizes.pieces, sizes.pieces)
    earlier = ones_where(iota(square, 0) < iota(square, 1))
    rank = dot(ones_where(place > 0), earlier)
    shape = (2 * sizes.owners, sizes.slots)
    source = iota(shape, 0)
    source = turn(sizes, over(source, sizes.owners), within(source, sizes.owners))
    offset = iota(shape, 1) - source * sizes.message
    spot = jnp.zeros(shape, F32)
    for each in range(sizes.cap):
        held = jnp.sum(jnp.where(rank == each, place, 0.0), axis=1, keepdims=True)
        spot = jnp.where(offset == each, held, spot)
    return jnp.sum(spot, axis=0, keepdims=True).astype(jnp.int32) - 1


def take_matrix(sizes, places):
    return ones_where(over(iota((sizes.width, sizes.slots), 0), sizes.sub) == places)


def coupled_inverse(sizes, level, limits, inverse, coupling):
    return dot(keep_live(limits, level, coupling, 1), inverse).astype(BF16)


def squared_inverse(sizes, level, limits, inverse):
    product = trans_dot(inverse, keep_live(limits, level, inverse, 0))
    return keep_live(limits, level, product, 1).astype(BF16)


def solve_forward(sizes, level, limits, residual, inverse):
    return keep_live(limits, level, dot_trans(residual, inverse[...]), 1).astype(BF16)


def solve_back(sizes, level, limits, solved, inverse):
    return keep_live(limits, level, dot(solved, inverse[...]), 1).astype(BF16)


def fetch(source, target, semaphore):
    copy = pltpu.make_async_copy(source, target, semaphore)
    copy.start()
    return copy


def send_pieces(sizes, sender, pieces):
    return dot_trans(sender, to_flat(sizes, pieces.astype(BF16))).astype(BF16)


def start_kernel(sizes, right, inverse, coupling, widths, targets, buffer, forward, limits, *refs):
    right_in, targets_in, send, next_send, next_take, product = refs[:6]
    held, below, widths_in, done = refs[6:-3], refs[-3], refs[-2], refs[-1]
    held = (*held[:3], below, *held[3:])
    copies = [
        fetch(targets, targets_in, done.at[0]),
        fetch(right.at[0, 0], right_in, done.at[1]),
        fetch(widths.at[0, 0], widths_in, done.at[2]),
    ]
    for at, target in enumerate(held):
        copies.append(fetch((inverse, coupling)[at % 2].at[0, 0, at // 2], target, done.at[3 + at]))
    copies[0].wait()
    slots = send_slots(sizes, 0, targets_in)
    send[...] = slots
    sender = send_matrix(sizes, slots)
    copies[1].wait()
    copies[2].wait()
    for level in range(sizes.levels):
        limits[level] = jnp.full((1, LANES), widths_in[level] * BLOCK, jnp.int32)
    for copy in copies[3:5]:
        copy.wait()
    next_send[...] = send_slots(sizes, 1, targets_in)
    next_take[...] = take_places(sizes, 0, targets_in)
    solved = solve_forward(sizes, 0, limits, right_in[0], held[0])
    forward[...] = solved
    pieces = dot_trans(solved, held[1][...])
    for copy in copies[5:7]:
        copy.wait()
    product[...] = coupled_inverse(sizes, 1, limits, held[2][...], held[3][...])
    buffer[...] = send_pieces(sizes, sender, pieces)
    for copy in copies[7:]:
        copy.wait()


def residual_of(sizes, level, arrived, right, taker):
    incoming = to_rows(sizes, dot_trans(arrived[...].T, taker))
    return (right[level].astype(F32) - incoming).astype(BF16)


def up_kernel(sizes, level, arrived, right, limits, targets, product, inverse, send, take, *refs):
    block, below, buffer, start, next_take, next_product, *more = refs
    next_take[...] = take_places(sizes, level, targets)
    following = (level + 1) % (sizes.levels - 1)
    if following:
        more[0][...] = send_slots(sizes, following, targets)
    residual = residual_of(sizes, level, arrived, right, take_matrix(sizes, take[...]))
    pieces = dot_trans(residual, product[...])
    next_product[...] = coupled_inverse(sizes, following, limits, block[...], below[...])
    solved = solve_forward(sizes, level, limits, residual, inverse)
    buffer[...] = send_pieces(sizes, send_matrix(sizes, send[...]), pieces)
    start[...] = solve_back(sizes, level, limits, solved, inverse)


def top_kernel(sizes, level, arrived, right, limits, inverse, take, forward, first, buffer, solution, start):
    taker = take_matrix(sizes, take[...])
    solved = solve_forward(sizes, level, limits, residual_of(sizes, level, arrived, right, taker), inverse)
    start[...] = solve_back(sizes, 0, limits, forward[...], first)
    value = solve_back(sizes, level, limits, solved, inverse)
    buffer[...] = cross_dot(taker, to_flat(sizes, value)).astype(BF16)
    solution[...] = value


def solution_of(sizes, level, arrived, start, product, send, limits):
    gathered = to_rows(sizes, dot(arrived[...].T, send_matrix(sizes, send[...]))).astype(BF16)
    update = keep_live(limits, level, dot(gathered, product[...]), 1)
    return (start[...].astype(F32) - update).astype(BF16)


def down_kernel(sizes, level, arrived, start, product, send, limits, take, buffer, solved):
    value = solution_of(sizes, level, arrived, start, product, send, limits)
    buffer[...] = dot(to_flat(sizes, value), take_matrix(sizes, take[...])).astype(BF16).T
    solved[...] = value


def last_kernel(sizes, arrived, start, product, send, limits, *refs):
    above, out, held, done = refs[:-3], refs[-3], refs[-2], refs[-1]
    copies = [fetch(solved, out.at[0, 0, at + 1], done.at[at + 1]) for at, solved in enumerate(above)]
    held[...] = solution_of(sizes, 0, arrived, start, product, send, limits)
    copies.append(fetch(held, out.at[0, 0, 0], done.at[0]))
    for copy in copies:
        copy.wait()


VMEM = pl.BlockSpec(memory_space=pltpu.VMEM)
HBM = pl.BlockSpec(memory_space=pltpu.HBM)


def call(kernel, name, operands, far, outs, cost, scratch=(), out_spec=VMEM):
    held = [pltpu.with_memory_space_constraint(one, pltpu.HBM) for one in operands[:far]]
    operands = (*held, *operands[far:])
    return pl.pallas_call(
        kernel,
        in_specs=[HBM] * far + [VMEM] * (len(operands) - far),
        out_specs=[out_spec] * len(outs),
        out_shape=[jax.ShapeDtypeStruct(shape, kind) for shape, kind in outs],
        scratch_shapes=scratch,
        compiler_params=pltpu.CompilerParams(vmem_limit_bytes=24 * 2**20),
        cost_estimate=pl.CostEstimate(flops=cost, bytes_accessed=2**20, transcendentals=0),
        name=name,
    )(*operands)


def shards(leaf_axes, right_sides, inverses, couplings, widths, targets):
    right_sides = jnp.swapaxes(right_sides, 3, 4)
    sizes = Sizes(right_sides, couplings, targets, leaf_axes)
    width, slots, rows, columns, levels = sizes.width, sizes.slots, sizes.rows, sizes.columns, sizes.levels
    top = levels - 1
    vector = ((columns, width), BF16)
    message = ((slots, sizes.sub * columns), BF16)
    matrix = ((width, width), BF16)
    coupled = ((rows, width), BF16)
    send_row, take_row = ((1, rows), jnp.int32), ((1, slots), jnp.int32)
    small, large = 10**6, 10**9

    def exchange(buffer, level):
        order = turns(sizes, level % sizes.leaf_bits)
        blocks = buffer.reshape(slots // 2, 2, buffer.shape[1])
        axes = (*leaf_axes, "far", "near")
        moved = lax.all_to_all(blocks, axes, split_axis=0, concat_axis=0, tiled=True, axis_index_groups=order)
        return moved.reshape(buffer.shape)

    inputs = (right_sides, inverses, couplings, widths, targets)
    buffer, forward, limits, right, codes, send, next_send, take, product, *held = call(
        functools.partial(start_kernel, sizes),
        "start",
        inputs,
        5,
        (
            message,
            vector,
            ((levels, 1, LANES), jnp.int32),
            ((levels, columns, width), BF16),
            (targets.shape, jnp.int32),
            send_row,
            send_row,
            take_row,
            coupled,
            matrix,
            coupled,
            matrix,
            *(matrix, coupled) * (top - 2),
            matrix,
        ),
        large,
        (pltpu.VMEM(*coupled), pltpu.SMEM((levels,), jnp.int32), pltpu.SemaphoreType.DMA((4 + 2 * top,))),
    )
    held.insert(3, None)
    blocks, below = held[::2], held[1::2]
    sends, takes, products, starts = [send, next_send], [take], [None, product], [None]
    for level in range(1, top):
        arrived = exchange(buffer, level - 1)
        following = (level + 1) % top
        buffer, start, take, product, *more = call(
            functools.partial(up_kernel, sizes, level),
            f"up_{level}",
            (arrived, right, limits, codes, products[level], blocks[level], sends[level], takes[-1], blocks[following], below[following]),
            0,
            (message, vector, take_row, coupled, *((send_row,) if following else ())),
            small,
        )
        starts.append(start)
        takes.append(take)
        sends.extend(more)
        products.append(product)
    arrived = exchange(buffer, top - 1)
    products[0] = products.pop()
    buffer, solved, starts[0] = call(
        functools.partial(top_kernel, sizes, top),
        "top",
        (arrived, right, limits, blocks[top], takes[-1], forward, blocks[0]),
        0,
        (message, vector, vector),
        small,
    )
    above = [solved]
    for level in reversed(range(1, top)):
        arrived = exchange(buffer, level)
        buffer, solved = call(
            functools.partial(down_kernel, sizes, level),
            f"down_{level}",
            (arrived, starts[level], products[level], sends[level], limits, takes[level - 1]),
            0,
            (message, vector),
            small,
        )
        above.insert(0, solved)
    arrived = exchange(buffer, 0)
    (out,) = call(
        functools.partial(last_kernel, sizes),
        "last",
        (arrived, starts[0], products[0], sends[0], limits, *above),
        0,
        ((right_sides.shape, BF16),),
        small,
        (pltpu.VMEM(*vector), pltpu.SemaphoreType.DMA((levels,))),
        HBM,
    )
    return jnp.swapaxes(out, 3, 4)


def solution(mesh):
    groups, owners = mesh.devices.shape
    bits = groups.bit_length() - 1
    near = 1 if owners % 4 else 4
    leaf_axes = tuple(f"leaf{bit}" for bit in reversed(range(bits)))
    split = Mesh(mesh.devices.reshape((2,) * bits + (owners // near, near)), leaf_axes + ("far", "near"))
    blk = ("far", "near")
    return jax.shard_map(
        functools.partial(shards, leaf_axes),
        mesh=split,
        in_specs=(
            P(leaf_axes, blk, None, None, None),
            P(leaf_axes, blk, None, None, None),
            P(leaf_axes, blk, None, None, None),
            P(leaf_axes, blk, None),
            P(),
        ),
        out_specs=P(leaf_axes, blk, None, None, None),
        check_vma=False,
    )
```

```python
import functools

import jax
import jax.numpy as jnp
from jax import lax
from jax.experimental import pallas as pl
from jax.experimental.pallas import tpu as pltpu
from jax.sharding import Mesh, PartitionSpec as P

BLOCK = 128
LANES = 128
F32 = jnp.float32
BF16 = jnp.bfloat16


def iota(shape, axis):
    return lax.broadcasted_iota(jnp.int32, shape, axis)


def ones_where(condition):
    return jnp.where(condition, 1.0, 0.0).astype(BF16)


def dot(left, right):
    return jnp.dot(left, right, preferred_element_type=F32)


def trans_dot(left, right):
    return lax.dot_general(left, right, (((0,), (0,)), ((), ())), preferred_element_type=F32)


def dot_trans(left, right):
    return lax.dot_general(left, right, (((1,), (1,)), ((), ())), preferred_element_type=F32)


def cross_dot(left, right):
    return lax.dot_general(left, right, (((0,), (1,)), ((), ())), preferred_element_type=F32)


def over(value, size):
    if size & (size - 1):
        return value // size
    return lax.shift_right_logical(value, size.bit_length() - 1)


def within(value, size):
    if size & (size - 1):
        return value % size
    return jnp.bitwise_and(value, size - 1)


class Sizes:
    def __init__(self, right_sides, couplings, targets, leaf_axes):
        self.leaf_axes = leaf_axes
        self.near, self.far = lax.axis_size("near"), lax.axis_size("far")
        self.owners = self.near * self.far
        self.levels, self.columns, self.width = right_sides.shape[-3:]
        self.rows = couplings.shape[-2]
        self.pieces = targets.shape[-1]
        self.leaf_bits = len(leaf_axes)
        self.sub = self.rows // self.pieces
        self.places = self.width // self.sub
        self.cap = max(3, (2 * self.pieces + self.owners - 1) // self.owners + 1)
        self.message = self.cap + self.cap % 2
        self.slots = 2 * self.owners * self.message


def keep_live(limits, level, value, axis):
    return jnp.where(iota(value.shape, axis) < limits[level][:, :1], value, jnp.zeros_like(value))


def keep_own(sizes, value):
    own = within(iota(value.shape, 1), sizes.sub) == over(iota(value.shape, 0), sizes.columns)
    return jnp.where(own, value, jnp.zeros_like(value))


def to_rows(sizes, value):
    value = keep_own(sizes, value)
    parts = [value[at * sizes.columns : (at + 1) * sizes.columns] for at in range(sizes.sub)]
    while len(parts) > 1:
        parts = [sum(parts[at : at + 2]) for at in range(0, len(parts), 2)]
    return parts[0]


def to_flat(sizes, value):
    return keep_own(sizes, jnp.concatenate([value] * sizes.sub, axis=0))


def position(sizes, level):
    group = 0
    for axis in sizes.leaf_axes:
        group = group * 2 + lax.axis_index(axis)
    owner = lax.axis_index("far") * sizes.near + lax.axis_index("near")
    return group, owner, level % sizes.leaf_bits


def turn(sizes, half, owner):
    at = (within(owner, sizes.near) * 2 + half) * sizes.far + over(owner, sizes.near)
    shift = 1
    while shift < 2 * sizes.owners:
        at = jnp.bitwise_xor(at, lax.shift_right_logical(at, shift))
        shift *= 2
    return at


def turns(sizes, bit):
    low = 2**bit
    order = []
    for group in range(2 ** sizes.leaf_bits):
        if group & low:
            continue
        members = []
        for at in range(2 * sizes.owners):
            at ^= at >> 1
            near, half, far = at // (2 * sizes.far), at // sizes.far % 2, at % sizes.far
            members.append((group + half * low) * sizes.owners + far * sizes.near + near)
        order.append(members)
    return order


def send_slots(sizes, level, targets):
    group, owner, bit = position(sizes, level)
    count = sizes.pieces
    table = targets[level, group]
    mine = jnp.sum(jnp.where(iota(table.shape, 0) == owner, table, 0), axis=0, keepdims=True)
    square = (count, count)
    keys_down = jnp.broadcast_to(over(mine, sizes.places), square)
    key_col = jnp.sum(jnp.where(iota(square, 0) == iota(square, 1), keys_down, 0).astype(F32), axis=1, keepdims=True)
    key_col = key_col.astype(jnp.int32)
    earlier = (keys_down == key_col) & (iota(square, 1) < iota(square, 0))
    rank = jnp.sum(jnp.where(earlier, 1.0, 0.0), axis=1, keepdims=True).astype(jnp.int32)
    side, dest = over(key_col, sizes.owners), within(key_col, sizes.owners)
    half = jnp.bitwise_xor(side, lax.shift_right_logical(group, bit) & 1)
    slot = turn(sizes, half, dest) * sizes.message + rank
    shape = (count, sizes.rows)
    chosen = over(iota(shape, 1), sizes.sub) == iota(shape, 0)
    return jnp.sum(jnp.where(chosen, slot, 0).astype(F32), axis=0, keepdims=True).astype(jnp.int32)


def send_matrix(sizes, slots):
    return ones_where(iota((sizes.slots, sizes.rows), 0) == slots)


def take_places(sizes, level, targets):
    group, owner, bit = position(sizes, level)
    own_half = lax.shift_right_logical(group, bit) & 1
    first = group - own_half * 2**bit
    tables = []
    for half in range(2):
        codes = targets[level, first + half * 2**bit]
        wanted = jnp.bitwise_xor(own_half, half) * sizes.owners + owner
        tables.append(jnp.where(over(codes, sizes.places) == wanted, within(codes, sizes.places) + 1, 0))
    place = jnp.concatenate(tables, axis=0).astype(F32)
    square = (sizes.pieces, sizes.pieces)
    earlier = ones_where(iota(square, 0) < iota(square, 1))
    rank = dot(ones_where(place > 0), earlier)
    shape = (2 * sizes.owners, sizes.slots)
    source = iota(shape, 0)
    source = turn(sizes, over(source, sizes.owners), within(source, sizes.owners))
    offset = iota(shape, 1) - source * sizes.message
    spot = jnp.zeros(shape, F32)
    for each in range(sizes.cap):
        held = jnp.sum(jnp.where(rank == each, place, 0.0), axis=1, keepdims=True)
        spot = jnp.where(offset == each, held, spot)
    return jnp.sum(spot, axis=0, keepdims=True).astype(jnp.int32) - 1


def take_matrix(sizes, places):
    return ones_where(over(iota((sizes.width, sizes.slots), 0), sizes.sub) == places)


def coupled_inverse(sizes, level, limits, inverse, coupling):
    return dot(keep_live(limits, level, coupling, 1), inverse).astype(BF16)


def squared_inverse(sizes, level, limits, inverse):
    product = trans_dot(inverse, keep_live(limits, level, inverse, 0))
    return keep_live(limits, level, product, 1).astype(BF16)


def solve_forward(sizes, level, limits, residual, inverse):
    return keep_live(limits, level, dot_trans(residual, inverse[...]), 1).astype(BF16)


def solve_back(sizes, level, limits, solved, inverse):
    return keep_live(limits, level, dot(solved, inverse[...]), 1).astype(BF16)


def fetch(source, target, semaphore):
    copy = pltpu.make_async_copy(source, target, semaphore)
    copy.start()
    return copy


def send_pieces(sizes, sender, pieces):
    return dot_trans(sender, to_flat(sizes, pieces.astype(BF16))).astype(BF16)


def start_kernel(sizes, right, inverse, coupling, widths, targets, buffer, forward, limits, *refs):
    right_in, targets_in, inverse_in, coupling_in, widths_in, done = refs
    first, others = pl.ds(0, 1), pl.ds(1, sizes.levels - 1)
    copies = [
        fetch(targets.at[first], targets_in.at[first], done.at[0]),
        fetch(right.at[0, 0, first], right_in.at[first], done.at[1]),
        fetch(widths.at[0, 0], widths_in, done.at[2]),
        fetch(inverse.at[0, 0, 0], inverse_in, done.at[3]),
        fetch(coupling.at[0, 0, 0], coupling_in, done.at[4]),
        fetch(right.at[0, 0, others], right_in.at[others], done.at[5]),
        fetch(targets.at[pl.ds(1, sizes.levels - 2)], targets_in.at[pl.ds(1, sizes.levels - 2)], done.at[6]),
    ]
    copies[0].wait()
    sender = send_matrix(sizes, send_slots(sizes, 0, targets_in))
    copies[1].wait()
    copies[2].wait()
    for level in range(sizes.levels):
        limits[level] = jnp.full((1, LANES), widths_in[level] * BLOCK, jnp.int32)
    copies[3].wait()
    solved = solve_forward(sizes, 0, limits, right_in[0], inverse_in)
    forward[...] = solved
    copies[4].wait()
    buffer[...] = send_pieces(sizes, sender, dot_trans(solved, coupling_in[...]))
    copies[5].wait()
    copies[6].wait()


def plan_kernel(sizes, inverse, coupling, forward, limits, targets, *refs):
    top = sizes.levels - 1
    sends, takes, start = refs[:3]
    products, blocks, square = refs[3 : 3 + top], refs[3 + top : 2 + 2 * top], refs[2 + 2 * top]
    first_in, top_in, coupling_in, done = refs[-4:]
    held = (first_in, *blocks, top_in)
    copies = []
    for level in (*range(1, top + 1), 0):
        at = 2 * len(copies)
        pair = [fetch(inverse.at[0, 0, level], held[level], done.at[at])]
        if level < top:
            pair.append(fetch(coupling.at[0, 0, level], coupling_in.at[level], done.at[at + 1]))
        copies.append(pair)
    for level in range(top):
        sends[level] = send_slots(sizes, level, targets)
        takes[level] = take_places(sizes, level, targets)
    for level in (*range(1, top + 1), 0):
        for copy in copies.pop(0):
            copy.wait()
        block = held[level][...]
        if level < top:
            products[level][...] = coupled_inverse(sizes, level, limits, block, coupling_in[level])
        else:
            square[...] = squared_inverse(sizes, level, limits, block)
    start[...] = solve_back(sizes, 0, limits, forward[...], first_in)


def residual_of(sizes, level, arrived, right, taker):
    incoming = to_rows(sizes, dot_trans(arrived[...].T, taker))
    return (right[level].astype(F32) - incoming).astype(BF16)


def up_kernel(sizes, level, arrived, right, product, inverse, sends, limits, takes, buffer, start):
    residual = residual_of(sizes, level, arrived, right, take_matrix(sizes, takes[level - 1]))
    pieces = dot_trans(residual, product[...])
    solved = solve_forward(sizes, level, limits, residual, inverse)
    buffer[...] = send_pieces(sizes, send_matrix(sizes, sends[level]), pieces)
    start[...] = solve_back(sizes, level, limits, solved, inverse)


def top_kernel(sizes, level, arrived, right, square, takes, buffer, solved):
    taker = take_matrix(sizes, takes[level - 1])
    value = dot(residual_of(sizes, level, arrived, right, taker), square[...]).astype(BF16)
    buffer[...] = cross_dot(taker, to_flat(sizes, value)).astype(BF16)
    solved[...] = value


def solution_of(sizes, level, arrived, start, product, sends, limits):
    gathered = to_rows(sizes, dot(arrived[...].T, send_matrix(sizes, sends[level]))).astype(BF16)
    update = keep_live(limits, level, dot(gathered, product[...]), 1)
    return (start[...].astype(F32) - update).astype(BF16)


def down_kernel(sizes, level, arrived, start, product, sends, limits, takes, buffer, solved):
    value = solution_of(sizes, level, arrived, start, product, sends, limits)
    taker = take_matrix(sizes, takes[level - 1])
    buffer[...] = dot(to_flat(sizes, value), taker).astype(BF16).T
    solved[...] = value


def last_kernel(sizes, arrived, start, product, sends, limits, *refs):
    above, out, held, done = refs[:-3], refs[-3], refs[-2], refs[-1]
    copies = [fetch(solved, out.at[0, 0, at + 1], done.at[at + 1]) for at, solved in enumerate(above)]
    held[...] = solution_of(sizes, 0, arrived, start, product, sends, limits)
    copies.append(fetch(held, out.at[0, 0, 0], done.at[0]))
    for copy in copies:
        copy.wait()


VMEM = pl.BlockSpec(memory_space=pltpu.VMEM)
HBM = pl.BlockSpec(memory_space=pltpu.HBM)


def call(kernel, name, operands, far, outs, cost, scratch=(), out_spec=VMEM):
    held = [pltpu.with_memory_space_constraint(one, pltpu.HBM) for one in operands[:far]]
    operands = (*held, *operands[far:])
    return pl.pallas_call(
        kernel,
        in_specs=[HBM] * far + [VMEM] * (len(operands) - far),
        out_specs=[out_spec] * len(outs),
        out_shape=[jax.ShapeDtypeStruct(shape, kind) for shape, kind in outs],
        scratch_shapes=scratch,
        compiler_params=pltpu.CompilerParams(vmem_limit_bytes=24 * 2**20),
        cost_estimate=pl.CostEstimate(flops=cost, bytes_accessed=2**20, transcendentals=0),
        name=name,
    )(*operands)


def shards(leaf_axes, right_sides, inverses, couplings, widths, targets):
    right_sides = jnp.swapaxes(right_sides, 3, 4)
    sizes = Sizes(right_sides, couplings, targets, leaf_axes)
    width, slots, rows, columns, levels = sizes.width, sizes.slots, sizes.rows, sizes.columns, sizes.levels
    top = levels - 1
    vector = ((columns, width), BF16)
    message = ((slots, sizes.sub * columns), BF16)
    matrix = ((width, width), BF16)
    coupled = ((rows, width), BF16)
    small, large = 10**6, 10**9

    def exchange(buffer, level):
        order = turns(sizes, level % sizes.leaf_bits)
        blocks = buffer.reshape(slots // 2, 2, buffer.shape[1])
        axes = (*leaf_axes, "far", "near")
        moved = lax.all_to_all(blocks, axes, split_axis=0, concat_axis=0, tiled=True, axis_index_groups=order)
        return moved.reshape(buffer.shape)

    inputs = (right_sides, inverses, couplings, widths, targets)
    buffer, *held = call(
        functools.partial(start_kernel, sizes),
        "start",
        inputs,
        5,
        (
            message,
            vector,
            ((levels, 1, LANES), jnp.int32),
            ((levels, columns, width), BF16),
            (targets.shape, jnp.int32),
        ),
        large,
        (
            pltpu.VMEM(*matrix),
            pltpu.VMEM(*coupled),
            pltpu.SMEM((levels,), jnp.int32),
            pltpu.SemaphoreType.DMA((7,)),
        ),
    )
    forward, limits, right, codes = held
    sends, takes, start, *planned = call(
        functools.partial(plan_kernel, sizes),
        "plan",
        (inverses, couplings, forward, limits, codes),
        2,
        (((top, 1, rows), jnp.int32), ((top, 1, slots), jnp.int32), vector, *(coupled,) * top, *(matrix,) * top),
        large,
        (
            pltpu.VMEM(*matrix),
            pltpu.VMEM(*matrix),
            pltpu.VMEM((top, rows, width), BF16),
            pltpu.SemaphoreType.DMA((2 * levels,)),
        ),
    )
    products, blocks = planned[:top], planned[top:]
    starts = [start]
    for level in range(1, top):
        arrived = exchange(buffer, level - 1)
        buffer, start = call(
            functools.partial(up_kernel, sizes, level),
            f"up_{level}",
            (arrived, right, products[level], blocks[level - 1], sends, limits, takes),
            0,
            (message, vector),
            small,
        )
        starts.append(start)
    arrived = exchange(buffer, top - 1)
    buffer, solved = call(
        functools.partial(top_kernel, sizes, top),
        "top",
        (arrived, right, blocks[-1], takes),
        0,
        (message, vector),
        small,
    )
    above = [solved]
    for level in reversed(range(1, top)):
        arrived = exchange(buffer, level)
        buffer, solved = call(
            functools.partial(down_kernel, sizes, level),
            f"down_{level}",
            (arrived, starts[level], products[level], sends, limits, takes),
            0,
            (message, vector),
            small,
        )
        above.insert(0, solved)
    arrived = exchange(buffer, 0)
    (out,) = call(
        functools.partial(last_kernel, sizes),
        "last",
        (arrived, starts[0], products[0], sends, limits, *above),
        0,
        ((right_sides.shape, BF16),),
        small,
        (pltpu.VMEM(*vector), pltpu.SemaphoreType.DMA((levels,))),
        HBM,
    )
    return jnp.swapaxes(out, 3, 4)


def solution(mesh):
    groups, owners = mesh.devices.shape
    bits = groups.bit_length() - 1
    near = 1 if owners % 4 else 4
    leaf_axes = tuple(f"leaf{bit}" for bit in reversed(range(bits)))
    split = Mesh(mesh.devices.reshape((2,) * bits + (owners // near, near)), leaf_axes + ("far", "near"))
    blk = ("far", "near")
    return jax.shard_map(
        functools.partial(shards, leaf_axes),
        mesh=split,
        in_specs=(
            P(leaf_axes, blk, None, None, None),
            P(leaf_axes, blk, None, None, None),
            P(leaf_axes, blk, None, None, None),
            P(leaf_axes, blk, None),
            P(),
        ),
        out_specs=P(leaf_axes, blk, None, None, None),
        check_vma=False,
    )
```

```python
import functools

import jax
import jax.numpy as jnp
from jax import lax
from jax.experimental import pallas as pl
from jax.experimental.pallas import tpu as pltpu
from jax.sharding import Mesh, PartitionSpec as P

BLOCK = 128
LANES = 128
F32 = jnp.float32
BF16 = jnp.bfloat16


def iota(shape, axis):
    return lax.broadcasted_iota(jnp.int32, shape, axis)


def ones_where(condition):
    return jnp.where(condition, 1.0, 0.0).astype(BF16)


def dot(left, right):
    return jnp.dot(left, right, preferred_element_type=F32)


def trans_dot(left, right):
    return lax.dot_general(left, right, (((0,), (0,)), ((), ())), preferred_element_type=F32)


def dot_trans(left, right):
    return lax.dot_general(left, right, (((1,), (1,)), ((), ())), preferred_element_type=F32)


def cross_dot(left, right):
    return lax.dot_general(left, right, (((0,), (1,)), ((), ())), preferred_element_type=F32)


def over(value, size):
    if size & (size - 1):
        return value // size
    return lax.shift_right_logical(value, size.bit_length() - 1)


def within(value, size):
    if size & (size - 1):
        return value % size
    return jnp.bitwise_and(value, size - 1)


class Sizes:
    def __init__(self, right_sides, couplings, targets, leaf_axes):
        self.leaf_axes = leaf_axes
        self.near, self.far = lax.axis_size("near"), lax.axis_size("far")
        self.owners = self.near * self.far
        self.levels, self.columns, self.width = right_sides.shape[-3:]
        self.rows = couplings.shape[-2]
        self.pieces = targets.shape[-1]
        self.leaf_bits = len(leaf_axes)
        self.sub = self.rows // self.pieces
        self.places = self.width // self.sub
        self.cap = max(3, (2 * self.pieces + self.owners - 1) // self.owners + 1)
        self.message = self.cap + self.cap % 2
        self.slots = 2 * self.owners * self.message


def keep_live(limits, level, value, axis):
    return jnp.where(iota(value.shape, axis) < limits[level][:, :1], value, jnp.zeros_like(value))


def keep_own(sizes, value):
    own = within(iota(value.shape, 1), sizes.sub) == over(iota(value.shape, 0), sizes.columns)
    return jnp.where(own, value, jnp.zeros_like(value))


def to_rows(sizes, value):
    value = keep_own(sizes, value)
    parts = [value[at * sizes.columns : (at + 1) * sizes.columns] for at in range(sizes.sub)]
    while len(parts) > 1:
        parts = [sum(parts[at : at + 2]) for at in range(0, len(parts), 2)]
    return parts[0]


def to_flat(sizes, value):
    return keep_own(sizes, jnp.concatenate([value] * sizes.sub, axis=0))


def position(sizes, level):
    group = 0
    for axis in sizes.leaf_axes:
        group = group * 2 + lax.axis_index(axis)
    owner = lax.axis_index("far") * sizes.near + lax.axis_index("near")
    return group, owner, level % sizes.leaf_bits


def turn(sizes, half, owner):
    at = (within(owner, sizes.near) * 2 + half) * sizes.far + over(owner, sizes.near)
    shift = 1
    while shift < 2 * sizes.owners:
        at = jnp.bitwise_xor(at, lax.shift_right_logical(at, shift))
        shift *= 2
    return at


def turns(sizes, bit):
    low = 2**bit
    order = []
    for group in range(2 ** sizes.leaf_bits):
        if group & low:
            continue
        members = []
        for at in range(2 * sizes.owners):
            at ^= at >> 1
            near, half, far = at // (2 * sizes.far), at // sizes.far % 2, at % sizes.far
            members.append((group + half * low) * sizes.owners + far * sizes.near + near)
        order.append(members)
    return order


def send_slots(sizes, level, targets):
    group, owner, bit = position(sizes, level)
    count = sizes.pieces
    table = targets[level, group]
    mine = jnp.sum(jnp.where(iota(table.shape, 0) == owner, table, 0), axis=0, keepdims=True)
    square = (count, count)
    keys_down = jnp.broadcast_to(over(mine, sizes.places), square)
    key_col = jnp.sum(jnp.where(iota(square, 0) == iota(square, 1), keys_down, 0).astype(F32), axis=1, keepdims=True)
    key_col = key_col.astype(jnp.int32)
    earlier = (keys_down == key_col) & (iota(square, 1) < iota(square, 0))
    rank = jnp.sum(jnp.where(earlier, 1.0, 0.0), axis=1, keepdims=True).astype(jnp.int32)
    side, dest = over(key_col, sizes.owners), within(key_col, sizes.owners)
    half = jnp.bitwise_xor(side, lax.shift_right_logical(group, bit) & 1)
    slot = turn(sizes, half, dest) * sizes.message + rank
    shape = (count, sizes.rows)
    chosen = over(iota(shape, 1), sizes.sub) == iota(shape, 0)
    return jnp.sum(jnp.where(chosen, slot, 0).astype(F32), axis=0, keepdims=True).astype(jnp.int32)


def send_matrix(sizes, slots):
    return ones_where(iota((sizes.slots, sizes.rows), 0) == slots)


def take_places(sizes, level, targets):
    group, owner, bit = position(sizes, level)
    own_half = lax.shift_right_logical(group, bit) & 1
    first = group - own_half * 2**bit
    tables = []
    for half in range(2):
        codes = targets[level, first + half * 2**bit]
        wanted = jnp.bitwise_xor(own_half, half) * sizes.owners + owner
        tables.append(jnp.where(over(codes, sizes.places) == wanted, within(codes, sizes.places) + 1, 0))
    place = jnp.concatenate(tables, axis=0).astype(F32)
    square = (sizes.pieces, sizes.pieces)
    earlier = ones_where(iota(square, 0) < iota(square, 1))
    rank = dot(ones_where(place > 0), earlier)
    shape = (2 * sizes.owners, sizes.slots)
    source = iota(shape, 0)
    source = turn(sizes, over(source, sizes.owners), within(source, sizes.owners))
    offset = iota(shape, 1) - source * sizes.message
    spot = jnp.zeros(shape, F32)
    for each in range(sizes.cap):
        held = jnp.sum(jnp.where(rank == each, place, 0.0), axis=1, keepdims=True)
        spot = jnp.where(offset == each, held, spot)
    return jnp.sum(spot, axis=0, keepdims=True).astype(jnp.int32) - 1


def take_matrix(sizes, places):
    return ones_where(over(iota((sizes.width, sizes.slots), 0), sizes.sub) == places)


def coupled_inverse(sizes, level, limits, inverse, coupling):
    return dot(keep_live(limits, level, coupling, 1), inverse).astype(BF16)


def squared_inverse(sizes, level, limits, inverse):
    product = trans_dot(inverse, keep_live(limits, level, inverse, 0))
    return keep_live(limits, level, product, 1).astype(BF16)


def solve_forward(sizes, level, limits, residual, inverse):
    return keep_live(limits, level, dot_trans(residual, inverse[...]), 1).astype(BF16)


def solve_back(sizes, level, limits, solved, inverse):
    return keep_live(limits, level, dot(solved, inverse[...]), 1).astype(BF16)


def fetch(source, target, semaphore):
    copy = pltpu.make_async_copy(source, target, semaphore)
    copy.start()
    return copy


def send_pieces(sizes, sender, pieces):
    return dot_trans(sender, to_flat(sizes, pieces.astype(BF16))).astype(BF16)


def start_kernel(sizes, right, inverse, coupling, widths, targets, buffer, forward, limits, *refs):
    right_in, targets_in, send, next_send, next_take, product = refs[:6]
    held, below, widths_in, done = refs[6:-3], refs[-3], refs[-2], refs[-1]
    held = (*held[:3], below, *held[3:])
    copies = [
        fetch(targets, targets_in, done.at[0]),
        fetch(right.at[0, 0], right_in, done.at[1]),
        fetch(widths.at[0, 0], widths_in, done.at[2]),
    ]
    for at, target in enumerate(held):
        copies.append(fetch((inverse, coupling)[at % 2].at[0, 0, at // 2], target, done.at[3 + at]))
    copies[0].wait()
    slots = send_slots(sizes, 0, targets_in)
    send[...] = slots
    sender = send_matrix(sizes, slots)
    copies[1].wait()
    copies[2].wait()
    for level in range(sizes.levels):
        limits[level] = jnp.full((1, LANES), widths_in[level] * BLOCK, jnp.int32)
    for copy in copies[3:5]:
        copy.wait()
    next_send[...] = send_slots(sizes, 1, targets_in)
    next_take[...] = take_places(sizes, 0, targets_in)
    solved = solve_forward(sizes, 0, limits, right_in[0], held[0])
    forward[...] = solved
    pieces = dot_trans(solved, held[1][...])
    for copy in copies[5:7]:
        copy.wait()
    product[...] = coupled_inverse(sizes, 1, limits, held[2][...], held[3][...])
    buffer[...] = send_pieces(sizes, sender, pieces)
    for copy in copies[7:]:
        copy.wait()


def residual_of(sizes, level, arrived, right, taker):
    incoming = to_rows(sizes, dot_trans(arrived[...].T, taker))
    return (right[level].astype(F32) - incoming).astype(BF16)


def up_kernel(sizes, level, arrived, right, limits, targets, product, inverse, send, take, *refs):
    block, below, buffer, start, next_take, next_product, *more = refs
    next_take[...] = take_places(sizes, level, targets)
    following = (level + 1) % (sizes.levels - 1)
    if following:
        more[0][...] = send_slots(sizes, following, targets)
    residual = residual_of(sizes, level, arrived, right, take_matrix(sizes, take[...]))
    pieces = dot_trans(residual, product[...])
    next_product[...] = coupled_inverse(sizes, following, limits, block[...], below[...])
    solved = solve_forward(sizes, level, limits, residual, inverse)
    buffer[...] = send_pieces(sizes, send_matrix(sizes, send[...]), pieces)
    start[...] = solve_back(sizes, level, limits, solved, inverse)


def top_kernel(sizes, level, arrived, right, limits, inverse, take, forward, first, buffer, solution, start):
    taker = take_matrix(sizes, take[...])
    solved = solve_forward(sizes, level, limits, residual_of(sizes, level, arrived, right, taker), inverse)
    value = solve_back(sizes, level, limits, solved, inverse)
    solution[...] = value
    start[...] = solve_back(sizes, 0, limits, forward[...], first)
    buffer[...] = cross_dot(taker, to_flat(sizes, value)).astype(BF16)


def solution_of(sizes, level, arrived, start, product, send, limits):
    gathered = to_rows(sizes, dot(arrived[...].T, send_matrix(sizes, send[...]))).astype(BF16)
    update = keep_live(limits, level, dot(gathered, product[...]), 1)
    return (start[...].astype(F32) - update).astype(BF16)


def down_kernel(sizes, level, arrived, start, product, send, limits, take, buffer, solved):
    value = solution_of(sizes, level, arrived, start, product, send, limits)
    buffer[...] = dot(to_flat(sizes, value), take_matrix(sizes, take[...])).astype(BF16).T
    solved[...] = value


def last_kernel(sizes, arrived, start, product, send, limits, *refs):
    above, out, held, done = refs[:-3], refs[-3], refs[-2], refs[-1]
    copies = [fetch(solved, out.at[0, 0, at + 1], done.at[at + 1]) for at, solved in enumerate(above)]
    held[...] = solution_of(sizes, 0, arrived, start, product, send, limits)
    copies.append(fetch(held, out.at[0, 0, 0], done.at[0]))
    for copy in copies:
        copy.wait()


VMEM = pl.BlockSpec(memory_space=pltpu.VMEM)
HBM = pl.BlockSpec(memory_space=pltpu.HBM)


def call(kernel, name, operands, far, outs, cost, scratch=(), out_spec=VMEM):
    held = [pltpu.with_memory_space_constraint(one, pltpu.HBM) for one in operands[:far]]
    operands = (*held, *operands[far:])
    return pl.pallas_call(
        kernel,
        in_specs=[HBM] * far + [VMEM] * (len(operands) - far),
        out_specs=[out_spec] * len(outs),
        out_shape=[jax.ShapeDtypeStruct(shape, kind) for shape, kind in outs],
        scratch_shapes=scratch,
        compiler_params=pltpu.CompilerParams(vmem_limit_bytes=24 * 2**20),
        cost_estimate=pl.CostEstimate(flops=cost, bytes_accessed=2**20, transcendentals=0),
        name=name,
    )(*operands)


def shards(leaf_axes, right_sides, inverses, couplings, widths, targets):
    right_sides = jnp.swapaxes(right_sides, 3, 4)
    sizes = Sizes(right_sides, couplings, targets, leaf_axes)
    width, slots, rows, columns, levels = sizes.width, sizes.slots, sizes.rows, sizes.columns, sizes.levels
    top = levels - 1
    vector = ((columns, width), BF16)
    message = ((slots, sizes.sub * columns), BF16)
    matrix = ((width, width), BF16)
    coupled = ((rows, width), BF16)
    send_row, take_row = ((1, rows), jnp.int32), ((1, slots), jnp.int32)
    small, large = 10**6, 10**9

    def exchange(buffer, level):
        order = turns(sizes, level % sizes.leaf_bits)
        blocks = buffer.reshape(slots // 2, 2, buffer.shape[1])
        axes = (*leaf_axes, "far", "near")
        moved = lax.all_to_all(blocks, axes, split_axis=0, concat_axis=0, tiled=True, axis_index_groups=order)
        return moved.reshape(buffer.shape)

    inputs = (right_sides, inverses, couplings, widths, targets)
    buffer, forward, limits, right, codes, send, next_send, take, product, *held = call(
        functools.partial(start_kernel, sizes),
        "start",
        inputs,
        5,
        (
            message,
            vector,
            ((levels, 1, LANES), jnp.int32),
            ((levels, columns, width), BF16),
            (targets.shape, jnp.int32),
            send_row,
            send_row,
            take_row,
            coupled,
            matrix,
            coupled,
            matrix,
            *(matrix, coupled) * (top - 2),
            matrix,
        ),
        large,
        (pltpu.VMEM(*coupled), pltpu.SMEM((levels,), jnp.int32), pltpu.SemaphoreType.DMA((4 + 2 * top,))),
    )
    held.insert(3, None)
    blocks, below = held[::2], held[1::2]
    sends, takes, products, starts = [send, next_send], [take], [None, product], [None]
    for level in range(1, top):
        arrived = exchange(buffer, level - 1)
        following = (level + 1) % top
        buffer, start, take, product, *more = call(
            functools.partial(up_kernel, sizes, level),
            f"up_{level}",
            (arrived, right, limits, codes, products[level], blocks[level], sends[level], takes[-1], blocks[following], below[following]),
            0,
            (message, vector, take_row, coupled, *((send_row,) if following else ())),
            small,
        )
        starts.append(start)
        takes.append(take)
        sends.extend(more)
        products.append(product)
    arrived = exchange(buffer, top - 1)
    products[0] = products.pop()
    buffer, solved, starts[0] = call(
        functools.partial(top_kernel, sizes, top),
        "top",
        (arrived, right, limits, blocks[top], takes[-1], forward, blocks[0]),
        0,
        (message, vector, vector),
        small,
    )
    above = [solved]
    for level in reversed(range(1, top)):
        arrived = exchange(buffer, level)
        buffer, solved = call(
            functools.partial(down_kernel, sizes, level),
            f"down_{level}",
            (arrived, starts[level], products[level], sends[level], limits, takes[level - 1]),
            0,
            (message, vector),
            small,
        )
        above.insert(0, solved)
    arrived = exchange(buffer, 0)
    (out,) = call(
        functools.partial(last_kernel, sizes),
        "last",
        (arrived, starts[0], products[0], sends[0], limits, *above),
        0,
        ((right_sides.shape, BF16),),
        small,
        (pltpu.VMEM(*vector), pltpu.SemaphoreType.DMA((levels,))),
        HBM,
    )
    return jnp.swapaxes(out, 3, 4)


def solution(mesh):
    groups, owners = mesh.devices.shape
    bits = groups.bit_length() - 1
    near = 1 if owners % 4 else 4
    leaf_axes = tuple(f"leaf{bit}" for bit in reversed(range(bits)))
    split = Mesh(mesh.devices.reshape((2,) * bits + (owners // near, near)), leaf_axes + ("far", "near"))
    blk = ("far", "near")
    return jax.shard_map(
        functools.partial(shards, leaf_axes),
        mesh=split,
        in_specs=(
            P(leaf_axes, blk, None, None, None),
            P(leaf_axes, blk, None, None, None),
            P(leaf_axes, blk, None, None, None),
            P(leaf_axes, blk, None),
            P(),
        ),
        out_specs=P(leaf_axes, blk, None, None, None),
        check_vma=False,
    )
```
